32 devices in a mesh: section: 2 (over x), dp: 4 (over z), tensor: 4 (over y, core).
Axes of the slice: x: 2, y: 2, z: 4, core: 2. Of those that a mesh axis runs over, the one named last changes fastest.
Arguments:
- images: bfloat16 [16, 196, 512], P('dp'), may hold values from -6 to 6
- out_grad: bfloat16 [16, 196, 512], P('dp'), may hold values from -6 to 6
- ln_gain: float32 [2, 2, 512], P('section'), may hold values from 0.5 to 1.5
- ln_bias: float32 [2, 2, 512], P('section'), may hold values from -2 to 2
- qkv_weight: bfloat16 [2, 3, 512, 512], P('section', None, None, 'tensor'), may hold values from -0.25 to 0.25
- qv_bias: float32 [2, 2, 512], P('section', None, 'tensor'), may hold values from -2 to 2
- pos_table: float32 [2, 169, 16], P('section', None, 'tensor'), may hold values from -4 to 4
- proj_weight: bfloat16 [2, 512, 512], P('section', 'tensor'), may hold values from -0.75 to 0.75
- out_bias: float32 [2, 2, 512], P('section'), may hold values from -2 to 2
- fc1_weight: bfloat16 [2, 512, 2048], P('section', None, 'tensor'), may hold values from -0.25 to 0.25
- fc1_bias: float32 [2, 2048], P('section', 'tensor'), may hold values from -2 to 2
- fc2_weight: bfloat16 [2, 2048, 512], P('section', 'tensor'), may hold values from -0.1875 to 0.1875
- rel_index: int32 [49, 49], replicated, may hold values from 0 to 168, as said below
- regions: int32 [14, 14], replicated, may hold values from 0 to 8, as said below
Outputs:
- section_out: bfloat16 [2, 16, 196, 512], P('section', 'dp')
- input_grad: float32 [2, 16, 196, 512], P('section', 'dp')
- grad_ln_gain: float32 [2, 2, 512], P('section')
- grad_ln_bias: float32 [2, 2, 512], P('section')
- grad_qkv_weight: float32 [2, 3, 512, 512], P('section', None, None, 'tensor')
- grad_qv_bias: float32 [2, 2, 512], P('section', None, 'tensor')
- grad_pos_table: float32 [2, 169, 16], P('section', None, 'tensor')
- grad_proj_weight: float32 [2, 512, 512], P('section', 'tensor')
- grad_out_bias: float32 [2, 2, 512], P('section')
- grad_fc1_weight: float32 [2, 512, 2048], P('section', None, 'tensor')
- grad_fc1_bias: float32 [2, 2048], P('section', 'tensor')
- grad_fc2_weight: float32 [2, 2048, 512], P('section', 'tensor')
The draws below stay inside these ranges and needn't reach their ends.
Inputs may be any that keep to these rules, and one draw needn't show every extreme that they name: rel_index[a, c] = p((row(a) - row(c) + 6) * 13 + column(a) - column(c) + 6) for a one-to-one map p of 0 to 168 onto itself, with row and column of a token inside its window. regions[i, j] = 3 * u(i) + v(j), where u and v split 0 to 13 into three nonempty runs of consecutive places numbered 0, 1, 2.
All inputs are finite; a program needn't handle non-finite values.
Results may differ from the reference program's by a relative error of at most 0.028.
Values may be sent and summed in bfloat16 or wider, within the bound.
No kernel may reach another device: no remote copies, remote signals or barrier semaphores. Data moves between devices by JAX's collectives and lax.ppermute only.
A program may use at most 128 MiB of HBM per device.

```python
import jax
import jax.numpy as jnp
from jax import lax

D = 512
HEADS = 16
HEAD_DIM = 32
FF = 2048
WIN = 7
SIDE = 14
SHIFT = 3
IMG_DEV = 4
IMAGES = 16
PIX = 196
WTOK = 49
NWIN = 4
REL = 169
BLOCKS = 2


def draw_rel_index(key, part):
    key = jax.random.fold_in(key, 11)
    extent = 2 * WIN - 1
    relabel = jax.random.permutation(key, extent * extent).astype(jnp.int32)
    places = jnp.arange(WIN * WIN, dtype=jnp.int32)
    row_of = places // WIN
    column_of = places % WIN
    relative = (row_of[:, None] - row_of[None, :] + WIN - 1) * extent + (column_of[:, None] - column_of[None, :] + WIN - 1)
    return relabel[relative]


def band_of(key):
    first_key, second_key = jax.random.split(key)
    first = jax.random.randint(first_key, (), 1, SIDE - 1)
    second = jax.random.randint(second_key, (), first + 1, SIDE)
    places = jnp.arange(SIDE, dtype=jnp.int32)
    return (places >= first).astype(jnp.int32) + (places >= second).astype(jnp.int32)


def draw_regions(key, part):
    key = jax.random.fold_in(key, 12)
    row_key, column_key = jax.random.split(key)
    return 3 * band_of(row_key)[:, None] + band_of(column_key)[None, :]


def levels(own_key, dims, cuts, low, top_value):
    factor_of = 1.0
    for position, shards_of in cuts:
        draws = jax.random.uniform(jax.random.fold_in(jax.random.fold_in(own_key, 6), position), (shards_of,), jnp.float32, low / len(cuts), top_value / len(cuts))
        factor_of = factor_of * jnp.repeat(jnp.exp(draws), dims[position] // shards_of).reshape((-1,) + (1,) * (len(dims) - 1 - position))
    return factor_of


def bell_draw(own_key, dims, scale, reach, cuts=(), kind=jnp.bfloat16):
    level = levels(own_key, dims, cuts, -0.22, 0.18) if cuts else 1.0
    drawn = jax.random.normal(own_key, dims, jnp.float32) * scale * level
    return jnp.minimum(jnp.maximum(drawn, -reach), reach).astype(kind)


def setup_inputs(seed: int = 0) -> dict:
    key_list = jax.random.split(jax.random.key(seed), 15)
    images = bell_draw(key_list[0], (IMAGES, PIX, D), 1.0, 6.0, ((0, 4),))
    out_grad = bell_draw(key_list[1], (IMAGES, PIX, D), 1.0, 6.0, ((0, 4),))
    ln_gain = jnp.clip(1.0 + 0.1 * jax.random.normal(key_list[2], (BLOCKS, 2, D), jnp.float32), 0.5, 1.5)
    ln_bias = bell_draw(key_list[3], (BLOCKS, 2, D), 0.3, 2.0, ((0, 2),), jnp.float32)
    qkv_weight = bell_draw(key_list[4], (BLOCKS, 3, D, D), D ** -0.5, 0.25, ((0, 2), (3, 4)))
    qv_bias = bell_draw(key_list[5], (BLOCKS, 2, D), 0.3, 2.0, ((0, 2), (2, 4)), jnp.float32)
    pos_table = bell_draw(key_list[6], (BLOCKS, REL, HEADS), 1.0, 4.0, ((0, 2), (2, 4)), jnp.float32)
    proj_weight = bell_draw(key_list[7], (BLOCKS, D, D), (D // 8) ** -0.5, 0.75, ((0, 2), (1, 4)))
    out_bias = bell_draw(key_list[8], (BLOCKS, 2, D), 0.3, 2.0, ((0, 2),), jnp.float32)
    fc1_weight = bell_draw(key_list[9], (BLOCKS, D, FF), D ** -0.5, 0.25, ((0, 2), (2, 4)))
    fc1_bias = bell_draw(key_list[10], (BLOCKS, FF), 0.3, 2.0, ((0, 2), (1, 4)), jnp.float32)
    fc2_weight = bell_draw(key_list[11], (BLOCKS, FF, D), (FF // 2) ** -0.5, 0.1875, ((0, 2), (1, 4)))
    rel_index = draw_rel_index(jax.random.fold_in(key_list[14], 71), 0)
    regions = draw_regions(jax.random.fold_in(key_list[14], 71), 0)
    return dict(images=images, out_grad=out_grad, ln_gain=ln_gain, ln_bias=ln_bias, qkv_weight=qkv_weight, qv_bias=qv_bias, pos_table=pos_table, proj_weight=proj_weight, out_bias=out_bias, fc1_weight=fc1_weight, fc1_bias=fc1_bias, fc2_weight=fc2_weight, rel_index=rel_index, regions=regions)


@jax.custom_vjp
def low(v):
    return lax.optimization_barrier(v.astype(jnp.bfloat16)).astype(jnp.float32)

@jax.custom_vjp
def low_back(v):
    return v

def low_keep(v):
    return (low(v), None)

def low_pass(kept, grad):
    return (grad,)

def back_keep(v):
    return (v, None)

def back_low(kept, grad):
    return (low(grad),)
low.defvjp(low_keep, low_pass)
low_back.defvjp(back_keep, back_low)
highest = lax.Precision.HIGHEST
epsilon = 1e-05

def layer_norm(values, gain, offset):
    center = values - lax.optimization_barrier(jnp.mean(values, -1, keepdims=True))
    spread = lax.optimization_barrier(jnp.mean(center * center, -1, keepdims=True))
    return center * lax.rsqrt(spread + epsilon) * gain + offset

def to_tiles(lattice):
    amount = lattice.shape[0]
    stripes = SIDE // WIN
    shaped = lattice.reshape(amount, stripes, WIN, stripes, WIN, lattice.shape[-1])
    return shaped.transpose(0, 1, 3, 2, 4, 5).reshape(amount, stripes * stripes, WIN * WIN, lattice.shape[-1])

def from_tiles(windowed):
    amount = windowed.shape[0]
    stripes = SIDE // WIN
    shaped = windowed.reshape(amount, stripes, stripes, WIN, WIN, windowed.shape[-1])
    return shaped.transpose(0, 1, 3, 2, 4, 5).reshape(amount, SIDE * SIDE, windowed.shape[-1])

def region_mask(regions):
    stripes = SIDE // WIN
    tiled = regions.reshape(stripes, WIN, stripes, WIN).transpose(0, 2, 1, 3).reshape(stripes * stripes, WIN * WIN)
    return jnp.where(tiled[:, :, None] != tiled[:, None, :], -100.0, 0.0).astype(jnp.float32)

def block(inputs, weights, rel_index, region_bias, offset):
    norm_gains, norm_shifts, qkv_w, qv_b, pos_bias, proj_w, out_b, fc1_w, fc1_b, fc2_w = weights
    amount = inputs.shape[0]
    lattice = jnp.roll(inputs.reshape(amount, SIDE, SIDE, D), (-offset, -offset), (1, 2))
    windowed = to_tiles(lattice.reshape(amount, PIX, D))
    normed = low(layer_norm(windowed, norm_gains[0], norm_shifts[0]))
    queries = low_back(low(jnp.einsum('nwtc,ce->nwte', normed, qkv_w[0], precision=highest) + qv_b[0]))
    keyed = low_back(low(jnp.einsum('nwtc,ce->nwte', normed, qkv_w[1], precision=highest)))
    values = low_back(low(jnp.einsum('nwtc,ce->nwte', normed, qkv_w[2], precision=highest) + qv_b[1]))
    heads_shape = windowed.shape[:-1] + (HEADS, HEAD_DIM)
    bias_terms = jnp.transpose(pos_bias[rel_index], (2, 0, 1))
    scores = jnp.einsum('nwahd,nwbhd->nwhab', queries.reshape(heads_shape), keyed.reshape(heads_shape), precision=highest) * HEAD_DIM ** (-0.5)
    scores = low_back(scores + bias_terms[None, None] + region_bias[None, :, None])
    soft_weights = low(jax.nn.softmax(scores, axis=-1))
    context = jnp.einsum('nwhab,nwbhd->nwahd', soft_weights, values.reshape(heads_shape), precision=highest)
    context = low_back(low(context.reshape(windowed.shape)))
    branch = low_back(jnp.einsum('nwte,ec->nwtc', context, proj_w, precision=highest) + out_b[0])
    middle = windowed + branch
    normed2 = low(layer_norm(middle, norm_gains[1], norm_shifts[1]))
    preact = low_back(jnp.einsum('nwtc,cf->nwtf', normed2, fc1_w, precision=highest) + fc1_b)
    hidden = low(jax.nn.gelu(preact, approximate=False))
    feedforward = low_back(jnp.einsum('nwtf,fc->nwtc', hidden, fc2_w, precision=highest) + out_b[1])
    result = from_tiles(middle + feedforward).reshape(amount, SIDE, SIDE, D)
    return jnp.roll(result, (offset, offset), (1, 2)).reshape(amount, PIX, D)

def reference(images, out_grad, ln_gain, ln_bias, qkv_weight, qv_bias, pos_table, proj_weight, out_bias, fc1_weight, fc1_bias, fc2_weight, rel_index, regions):
    weights = (ln_gain, ln_bias, qkv_weight.astype(jnp.float32), qv_bias, pos_table, proj_weight.astype(jnp.float32), out_bias, fc1_weight.astype(jnp.float32), fc1_bias, fc2_weight.astype(jnp.float32))
    plain_mask = jnp.zeros((NWIN, WTOK, WTOK), jnp.float32)
    rolled_mask = region_mask(regions)

    def forward(params, inputs, nudge):
        first = block(inputs, jax.tree.map(lambda weight: weight[0], params), rel_index, plain_mask, 0)
        second = block(low_back(low(first)) + nudge, jax.tree.map(lambda weight: weight[1], params), rel_index, rolled_mask, SHIFT)
        return (first, second)
    groups = IMAGES // IMG_DEV
    image_groups = images.astype(jnp.float32).reshape(groups, IMG_DEV, PIX, D)
    grad_groups = out_grad.astype(jnp.float32).reshape(groups, IMG_DEV, PIX, D)

    def one_group(totals, paired):
        inputs, cotangent = paired
        nudge = jnp.zeros_like(inputs)
        outputs, pull = jax.vjp(forward, weights, inputs, nudge)
        grad_weights, grad_inputs, grad_nudge = pull((jnp.zeros_like(outputs[0]), cotangent))
        totals = jax.tree.map(lambda left, right: left + right, totals, grad_weights)
        return (totals, (outputs[0], outputs[1], grad_inputs, grad_nudge))
    zeros = jax.tree.map(jnp.zeros_like, weights)
    totals, (first, second, grad_first, grad_second) = lax.scan(one_group, zeros, (image_groups, grad_groups))
    section_out = jnp.stack([first.reshape(IMAGES, PIX, D), second.reshape(IMAGES, PIX, D)]).astype(jnp.bfloat16)
    input_grad = jnp.stack([grad_first.reshape(IMAGES, PIX, D), grad_second.reshape(IMAGES, PIX, D)])
    return (section_out, input_grad, totals[0], totals[1], totals[2], totals[3], totals[4], totals[5], totals[6], totals[7], totals[8], totals[9])
```

```python
import functools

import jax
import jax.numpy as jnp
import numpy as np
from jax import lax
from jax.experimental import pallas as pl
from jax.experimental.pallas import tpu as pltpu
from jax.sharding import PartitionSpec as P

D = 512
HEAD_DIM = 32
WIN = 7
SIDE = 14
SHIFT = 3
PIX = 196
WTOK = 49
REL = 169
NWIN = 4

ROWS = 64
M = NWIN * ROWS
TOK = 208
GROUP = 4
LANES = GROUP * HEAD_DIM
WIDE = GROUP * ROWS
SLOTS = 4

EPS = 1e-05
SCALE = HEAD_DIM ** (-0.5)
BF = jnp.bfloat16
F32 = jnp.float32
HIGHEST = lax.Precision.HIGHEST

SEC, DP, TEN = "section", "dp", "tensor"

(
    X,
    NORMED,
    XHAT1,
    R1,
    CTX,
    MIDDLE,
    NORMED2,
    XHAT2,
    R2,
    HIDDEN,
    Y,
    GMLP,
    GPRE,
    GMIDDLE,
    GBRANCH,
    SUMS_B,
    GQKV,
    DOWN,
    SUMS_A,
    SCORESUM,
    PV,
    PERM,
    PERM_T,
    BIAS,
    REGION,
    FC1W,
    FC2W,
    PROBS,
    PROJW,
    QKV,
    QKVW,
    SLOPE,
) = range(32)


def dot(a, b, ca, cb):
    return lax.dot_general(a, b, (((ca,), (cb,)), ((), ())), preferred_element_type=F32)


class Env:
    def __init__(self, refs, copies_in, copies_out):
        self.refs, self.copies_in, self.copies_out = refs, dict(copies_in), dict(copies_out)
        self.started = []

    def __getitem__(self, name):
        return self.refs[name]

    def need(self, name):
        copy = self.copies_in.pop(name, None)
        if copy is not None:
            copy.wait()
        return self.refs[name]

    def emit(self, name):
        copy = self.copies_out.pop(name, None)
        if copy is not None:
            copy.start()
            self.started.append(copy)

    def finish(self):
        for name in list(self.copies_in):
            self.need(name)
        for name in list(self.copies_out):
            self.emit(name)
        for copy in self.started:
            copy.wait()


def head_masks():
    lane = lax.broadcasted_iota(jnp.int32, (1, LANES), 1) // HEAD_DIM
    return [(lane == h).astype(F32) for h in range(GROUP)]


def spread(rows, masks):
    return jnp.concatenate([rows * mask.astype(BF) for mask in masks], axis=0)


def gather_heads(stacked, masks):
    total = stacked[0:ROWS] * masks[0]
    for h in range(1, GROUP):
        total = total + stacked[h * ROWS : (h + 1) * ROWS] * masks[h]
    return total


def norm_of(values):
    center = values - jnp.mean(values, -1, keepdims=True)
    r = lax.rsqrt(jnp.mean(center * center, -1, keepdims=True) + EPS)
    return center * r, r


def joined_qkv(ref):
    return jnp.concatenate([ref[0], ref[1], ref[2]], axis=1)


def forward_attention(env):
    masks = head_masks()
    tiles = dot(env[PERM][...], env.need(X)[...], 1, 0)
    xhat, r = norm_of(tiles)
    env[XHAT1][...] = xhat
    env[R1][...] = jnp.broadcast_to(r, (M, 128))
    env.emit(XHAT1)
    env.emit(R1)
    normed = (xhat * env[PV][0:1, :] + env[PV][2:3, :]).astype(BF)
    env[NORMED][...] = normed
    env.emit(NORMED)
    branch = jnp.zeros((M, D), F32)
    for j in range(SLOTS):
        weight = joined_qkv(env.need((QKVW, j)))
        packed = (dot(normed, weight, 1, 0) + env[PV][12 + j : 13 + j, 0 : 3 * LANES]).astype(BF)
        env[(QKV, j)][...] = packed
        env.emit((QKV, j))
        parts = []
        for w in range(NWIN):
            rows = slice(w * ROWS, (w + 1) * ROWS)
            q = packed[rows, 0:LANES]
            k = packed[rows, LANES : 2 * LANES]
            v = packed[rows, 2 * LANES : 3 * LANES]
            scores = dot(k, spread(q, masks), 1, 1) * SCALE + env[BIAS][j] + env[REGION][w]
            exps = jnp.exp(scores - jnp.max(scores, 0, keepdims=True))
            probs = exps / jnp.sum(exps, 0, keepdims=True)
            env[(PROBS, j)][w] = probs
            parts.append(gather_heads(dot(probs.astype(BF), v, 0, 0), masks))
        env.emit((PROBS, j))
        context = jnp.concatenate(parts, axis=0).astype(BF)
        env[CTX][j] = context
        branch = branch + dot(context, env.need((PROJW, j))[...], 1, 0)
    env.emit(CTX)
    env[MIDDLE][...] = tiles + branch + env[PV][4:5, :]
    env.emit(MIDDLE)


def forward_mlp(env):
    middle = env.need(MIDDLE)[...]
    xhat, r = norm_of(middle)
    env[XHAT2][...] = xhat
    env[R2][...] = jnp.broadcast_to(r, (M, 128))
    env.emit(XHAT2)
    env.emit(R2)
    normed = (xhat * env[PV][1:2, :] + env[PV][3:4, :]).astype(BF)
    env[NORMED2][...] = normed
    env.emit(NORMED2)
    total = middle + env[PV][5:6, :]
    for j in range(SLOTS):
        pre = dot(normed, env.need((FC1W, j))[...], 1, 0) + env[PV][8 + j : 9 + j, :]
        phi = 0.5 * (1.0 + lax.erf(pre * (0.5**0.5)))
        hidden = (pre * phi).astype(BF)
        env[(SLOPE, j)][...] = phi + pre * jnp.exp(-0.5 * pre * pre) * (2.0 * np.pi) ** -0.5
        env.emit((SLOPE, j))
        env[HIDDEN][j] = hidden
        total = total + dot(hidden, env.need((FC2W, j))[...], 1, 0)
    env[Y][...] = dot(env[PERM_T][...], total.astype(BF), 1, 0).astype(BF)
    env.emit(Y)
    env.emit(HIDDEN)


def backward_norm(grad, xhat, r, gain):
    u = grad * gain
    return r * (u - jnp.mean(u, -1, keepdims=True) - xhat * jnp.mean(u * xhat, -1, keepdims=True))


def column_sum(values):
    return jnp.sum(values, 0, keepdims=True)


def backward_mlp(env):
    gmlp = env.need(GMLP)[...]
    gtiles = gmlp.astype(F32)
    sums = env[SUMS_B]
    sums[3:4, :] = column_sum(gtiles)
    total = jnp.zeros((M, D), F32)
    for j in range(SLOTS):
        gact = dot(gmlp, env.need((FC2W, j))[...], 1, 1)
        gpre = (gact * env.need((SLOPE, j))[...]).astype(BF)
        env[GPRE][j] = gpre
        sums[4 + j : 5 + j, :] = column_sum(gpre.astype(F32))
        total = total + dot(gpre, env.need((FC1W, j))[...], 1, 1)
    env.emit(GPRE)
    xhat = env.need(XHAT2)[...]
    r = env.need(R2)[:, 0:1]
    sums[0:1, :] = column_sum(total * xhat)
    sums[1:2, :] = column_sum(total)
    gmiddle = gtiles + backward_norm(total, xhat, r, env[PV][1:2, :])
    env[GMIDDLE][...] = gmiddle
    env.emit(GMIDDLE)
    gbranch = gmiddle.astype(BF)
    env[GBRANCH][...] = gbranch
    env.emit(GBRANCH)
    sums[2:3, :] = column_sum(gbranch.astype(F32))
    env.emit(SUMS_B)


def backward_attention(env):
    masks = head_masks()
    sums = env[SUMS_A]
    sums[...] = jnp.zeros_like(sums)
    gbranch = env.need(GBRANCH)[...]
    total = jnp.zeros((M, D), F32)
    for j in range(SLOTS):
        gcontext = dot(gbranch, env.need((PROJW, j))[...], 1, 1).astype(BF)
        packed = env.need((QKV, j))[...]
        env.need((PROBS, j))
        score_sum = None
        parts = []
        for w in range(NWIN):
            rows = slice(w * ROWS, (w + 1) * ROWS)
            q = spread(packed[rows, 0:LANES], masks)
            k = packed[rows, LANES : 2 * LANES]
            v = packed[rows, 2 * LANES : 3 * LANES]
            up = spread(gcontext[rows], masks)
            probs = env[(PROBS, j)][w]
            gprobs = dot(v, up, 1, 1)
            gscores = probs * (gprobs - jnp.sum(gprobs * probs, 0, keepdims=True))
            low = gscores.astype(BF)
            wide = low.astype(F32)
            score_sum = wide if score_sum is None else score_sum + wide
            gv = dot(probs.astype(BF), up, 1, 0)
            gk = dot(low, q, 1, 0) * SCALE
            gq = gather_heads(dot(low, k, 0, 0), masks) * SCALE
            parts.append(jnp.concatenate([gq, gk, gv], axis=1).astype(BF))
        env[SCORESUM][j] = score_sum
        grads = jnp.concatenate(parts, axis=0)
        env[GQKV][j] = grads
        sums[4 + j : 5 + j, 0 : 3 * LANES] = column_sum(grads.astype(F32))
        total = total + dot(grads, joined_qkv(env.need((QKVW, j))), 1, 1)
    env.emit(SCORESUM)
    env.emit(GQKV)
    xhat = env.need(XHAT1)[...]
    r = env.need(R1)[:, 0:1]
    sums[0:1, :] = column_sum(total * xhat)
    sums[1:2, :] = column_sum(total)
    env.emit(SUMS_A)
    down = env.need(GMIDDLE)[...] + backward_norm(total, xhat, r, env[PV][0:1, :])
    env[DOWN][...] = dot(env[PERM_T][...], down.astype(BF), 1, 0).astype(BF)
    env.emit(DOWN)


def shapes_of():
    table = {
        X: ((TOK, D), BF),
        NORMED: ((M, D), BF),
        XHAT1: ((M, D), F32),
        R1: ((M, 128), F32),
        CTX: ((SLOTS, M, LANES), BF),
        MIDDLE: ((M, D), F32),
        NORMED2: ((M, D), BF),
        XHAT2: ((M, D), F32),
        R2: ((M, 128), F32),
        HIDDEN: ((SLOTS, M, D), BF),
        Y: ((TOK, D), BF),
        GMLP: ((M, D), BF),
        GPRE: ((SLOTS, M, D), BF),
        GMIDDLE: ((M, D), F32),
        GBRANCH: ((M, D), BF),
        SUMS_B: ((8, D), F32),
        GQKV: ((SLOTS, M, 3 * LANES), BF),
        DOWN: ((TOK, D), BF),
        SUMS_A: ((8, D), F32),
        SCORESUM: ((SLOTS, ROWS, WIDE), F32),
    }
    for j in range(SLOTS):
        table[(QKVW, j)] = ((3, D, LANES), BF)
        table[(PROJW, j)] = ((LANES, D), BF)
        table[(FC1W, j)] = ((D, D), BF)
        table[(FC2W, j)] = ((D, D), BF)
        table[(QKV, j)] = ((M, 3 * LANES), BF)
        table[(PROBS, j)] = ((NWIN, ROWS, WIDE), F32)
        table[(SLOPE, j)] = ((M, D), F32)
    return table


SHAPES = shapes_of()


def per_slot(*names):
    return [(name, j) for j in range(SLOTS) for name in names]


ATT_WEIGHTS = per_slot(QKVW, PROJW)
MLP_WEIGHTS = per_slot(FC1W, FC2W)
ATT_OUT = [XHAT1, R1, NORMED] + per_slot(QKV, PROBS) + [CTX, MIDDLE]
MLP_OUT = [XHAT2, R2, NORMED2] + per_slot(SLOPE) + [Y, HIDDEN]
BACK_MLP_OUT = [GPRE, GMIDDLE, GBRANCH, SUMS_B]
BACK_ATT_OUT = [SCORESUM, GQKV, SUMS_A, DOWN]


def run_stages(stages, active, section, small, arrays, ins, outs, keep=(), scratch=()):
    small_names = list(small)
    kept = [name for name in outs if name in keep]
    n_small, n_in, n_kept, n_out = len(small_names), len(ins), len(kept), len(outs)
    local = [name for name in list(ins) + list(outs) + list(scratch)]

    def kernel(*refs):
        place = refs[0]
        at = 1
        env_refs = dict(zip(small_names, refs[at : at + n_small]))
        at += n_small
        in_hbm = refs[at : at + n_in]
        at += n_in + n_kept
        out_hbm = refs[at : at + n_out]
        at += n_out
        env_refs.update(zip(local, refs[at : at + len(local)]))
        sems = refs[at + len(local)]

        @pl.when(place[0] == active)
        def _():
            copies_in = {}
            for i, name in enumerate(ins):
                copies_in[name] = pltpu.make_async_copy(in_hbm[i], env_refs[name], sems.at[i])
                copies_in[name].start()
            copies_out = {
                name: pltpu.make_async_copy(env_refs[name], out_hbm[i], sems.at[n_in + i])
                for i, name in enumerate(outs)
            }
            env = Env(env_refs, copies_in, copies_out)
            for stage in stages:
                stage(env)
            env.finish()

    vmem = pl.BlockSpec(memory_space=pltpu.VMEM)
    hbm = pl.BlockSpec(memory_space=pl.ANY)
    results = pl.pallas_call(
        kernel,
        out_shape=[jax.ShapeDtypeStruct(*SHAPES[name]) for name in outs],
        in_specs=[pl.BlockSpec(memory_space=pltpu.SMEM)]
        + [vmem] * n_small
        + [hbm] * (n_in + n_kept),
        out_specs=[hbm] * n_out,
        scratch_shapes=[pltpu.VMEM(*SHAPES[name]) for name in local]
        + [pltpu.SemaphoreType.DMA((n_in + n_out,))],
        input_output_aliases={
            1 + n_small + n_in + i: outs.index(name) for i, name in enumerate(kept)
        },
        compiler_params=pltpu.CompilerParams(vmem_limit_bytes=48 * 1024 * 1024),
        cost_estimate=pl.CostEstimate(
            flops=5_000_000_000, bytes_accessed=8_000_000, transcendentals=1_000_000
        ),
    )(
        section,
        *[small[name] for name in small_names],
        *[arrays[name] for name in ins],
        *[arrays[name] for name in kept],
    )
    arrays.update(zip(outs, results))


def tile_places(shift):
    places = np.full((NWIN, ROWS), -1, np.int32)
    for w in range(NWIN):
        for r in range(WTOK):
            i = (w // 2) * WIN + r // WIN
            j = (w % 2) * WIN + r % WIN
            places[w, r] = ((i + shift) % SIDE) * SIDE + (j + shift) % SIDE
    return places.reshape(M)


def permutations(shifted):
    places = jnp.where(shifted, jnp.asarray(tile_places(SHIFT)), jnp.asarray(tile_places(0)))
    tokens = jnp.arange(TOK, dtype=jnp.int32)
    forth = (places[:, None] == tokens[None, :]).astype(BF)
    back = (tokens[:, None] == places[None, :]).astype(BF)
    return forth, back


def region_bias(regions, shifted):
    stripes = SIDE // WIN
    tiled = (
        regions.reshape(stripes, WIN, stripes, WIN)
        .transpose(0, 2, 1, 3)
        .reshape(stripes * stripes, WIN * WIN)
    )
    tiled = jnp.pad(tiled, ((0, 0), (0, ROWS - WTOK)))
    differ = (tiled[:, :, None] != tiled[:, None, :]) & shifted
    return jnp.tile(jnp.where(differ, -100.0, 0.0).astype(F32), (1, 1, GROUP))


def xor_permute(array, by):
    devices = lax.axis_size(TEN)
    return lax.ppermute(array, TEN, [(i, i ^ by) for i in range(devices)])


def gather_slots(array):
    across = xor_permute(array, 2)
    return [array, xor_permute(array, 1), across, xor_permute(across, 1)]


def section_permute(array, source):
    return lax.ppermute(array, SEC, [(source, 1 - source)])


def line_sum(part):
    devices = lax.axis_size(DP)
    if devices != 4:
        return lax.psum(part, DP)
    inner = lax.axis_index(DP)
    inner = (inner == 1) | (inner == 2)
    part = part + lax.ppermute(part, DP, [(0, 1), (3, 2)])
    part = part + lax.ppermute(part, DP, [(1, 2), (2, 1)])
    return jnp.where(inner, part, lax.ppermute(part, DP, [(1, 0), (2, 3)]))


def slot_sum(parts):
    near = xor_permute(jnp.stack([parts[1].astype(BF), parts[3].astype(BF)]), 1)
    far = (parts[2] + near[1].astype(F32)).astype(BF)
    far = xor_permute(far, 2)
    return (parts[0] + near[0].astype(F32) + far.astype(F32)).astype(BF)


def local(
    images,
    out_grad,
    ln_gain,
    ln_bias,
    qkv_weight,
    qv_bias,
    pos_table,
    proj_weight,
    out_bias,
    fc1_weight,
    fc1_bias,
    fc2_weight,
    rel_index,
    regions,
):
    section_id = lax.axis_index(SEC)
    shifted = section_id == 1
    section = section_id.astype(jnp.int32).reshape(1)
    tensor = lax.axis_index(TEN)

    pad = jnp.zeros((LANES,), F32)
    row = jnp.concatenate([qv_bias[0, 0], pad, qv_bias[0, 1], pad])
    table = jnp.pad(pos_table[0].reshape(-1), (0, 2 * D - REL * GROUP)).reshape(2, D)
    own_small = jnp.concatenate([fc1_bias[0][None], row[None], table], axis=0)
    small_slots = gather_slots(own_small)
    arrays = {}
    for name, own in (
        (QKVW, qkv_weight[0]),
        (PROJW, proj_weight[0]),
        (FC1W, fc1_weight[0]),
        (FC2W, fc2_weight[0]),
    ):
        for j, part in enumerate(gather_slots(own)):
            arrays[name, j] = part

    forth, back = permutations(shifted)
    rel = jnp.pad(rel_index, ((0, ROWS - WTOK), (0, ROWS - WTOK)), constant_values=-1)
    onehot = (rel.T[None] == jnp.arange(REL, dtype=jnp.int32)[:, None, None]).astype(F32)
    heads = jnp.stack([part[2:4].reshape(-1)[: REL * GROUP] for part in small_slots])
    heads = heads.reshape(SLOTS, REL, GROUP)
    bias = jnp.einsum("jrh,rca->jcha", heads, onehot, precision=HIGHEST)
    bias = bias.reshape(SLOTS, ROWS, WIDE)
    bias = jnp.where(jnp.arange(ROWS)[None, :, None] < WTOK, bias, -1e30)
    region = region_bias(regions, shifted)
    vectors = jnp.concatenate(
        [ln_gain[0], ln_bias[0], out_bias[0], jnp.zeros((2, D), F32)]
        + [part[0:1] for part in small_slots]
        + [part[1:2] for part in small_slots],
        axis=0,
    )
    all_small = {PV: vectors, PERM: forth, PERM_T: back, BIAS: bias, REGION: region}

    def small(*names):
        return {name: all_small[name] for name in names}

    images_each = images.shape[0] // lax.axis_size(TEN)

    def own_image(batch):
        one = lax.dynamic_slice_in_dim(batch, tensor * images_each, images_each, 0)
        return jnp.pad(one.reshape(PIX, D), ((0, TOK - PIX), (0, 0)))

    arrays[X] = own_image(images)
    run_stages(
        [forward_attention], 0, section, small(PV, PERM, BIAS, REGION),
        arrays, [X] + ATT_WEIGHTS, ATT_OUT,
    )
    run_stages(
        [forward_mlp], 0, section, small(PV, PERM_T),
        arrays, [MIDDLE] + MLP_WEIGHTS, MLP_OUT,
    )
    upstream = own_image(out_grad)
    arrays[X] = section_permute(arrays[Y], 0)
    arrays[GMLP] = dot(forth, upstream, 1, 0).astype(BF)
    outs = [NORMED, CTX, NORMED2, Y, HIDDEN, GPRE, GBRANCH, SUMS_B] + BACK_ATT_OUT
    saved = dict(arrays)
    run_stages(
        [forward_attention, forward_mlp, backward_mlp, backward_attention], 1, section,
        small(PV, PERM, PERM_T, BIAS, REGION),
        arrays, [X] + ATT_WEIGHTS + MLP_WEIGHTS + [GMLP], outs,
        keep=(NORMED, CTX, NORMED2, Y, HIDDEN),
        scratch=[XHAT1, R1, MIDDLE, XHAT2, R2, GMIDDLE]
        + per_slot(QKV, PROBS, SLOPE),
    )
    arrived = section_permute(arrays[DOWN], 1)
    gmlp = dot(forth, jnp.where(shifted, upstream, arrived), 1, 0).astype(BF)
    arrays[GMLP] = gmlp
    hidden = arrays[HIDDEN]
    fc2_parts = [dot(hidden[j], gmlp, 0, 0) for j in range(SLOTS)]
    fc2_grad = line_sum(slot_sum(fc2_parts))
    run_stages(
        [backward_mlp], 0, section, small(PV),
        arrays, [GMLP] + MLP_WEIGHTS + per_slot(SLOPE) + [XHAT2, R2], BACK_MLP_OUT,
        keep=(GPRE, GBRANCH, SUMS_B),
    )
    fc1_parts = [dot(arrays[NORMED2], arrays[GPRE][j], 0, 0) for j in range(SLOTS)]
    fc1_grad = line_sum(slot_sum(fc1_parts))
    run_stages(
        [backward_attention], 0, section, small(PV, PERM_T),
        arrays,
        [GBRANCH] + ATT_WEIGHTS + per_slot(QKV, PROBS) + [XHAT1, R1, GMIDDLE],
        BACK_ATT_OUT, keep=BACK_ATT_OUT,
    )
    sums_a, sums_b = arrays[SUMS_A], arrays[SUMS_B]
    scores = arrays[SCORESUM].reshape(SLOTS, ROWS, GROUP, ROWS)
    table_grad = jnp.einsum("jcha,rca->jrh", scores, onehot, precision=HIGHEST)
    table_grad = jnp.pad(table_grad.reshape(SLOTS, -1), ((0, 0), (0, 2 * D - REL * GROUP)))
    table_grad = table_grad.reshape(SLOTS, 2, D)
    shared = jnp.concatenate([sums_a[0:1], sums_b[0:1], sums_a[1:2], sums_b[1:2], sums_b[2:4]])
    tail_parts = []
    for j in range(SLOTS):
        qkv_part = dot(arrays[NORMED], arrays[GQKV][j], 0, 0)
        proj_part = dot(arrays[CTX][j], arrays[GBRANCH], 0, 0)
        rows = jnp.concatenate(
            [proj_part, shared, sums_b[4 + j : 5 + j], sums_a[4 + j : 5 + j], table_grad[j]]
            + [jnp.zeros((6, D), F32)]
        )
        tail_parts.append((qkv_part, rows))
    qkv_grad = line_sum(slot_sum([part[0] for part in tail_parts]))
    rest = line_sum(slot_sum([part[1] for part in tail_parts]))

    def spread_images(own):
        mine, near, far, both = gather_slots(own[:PIX])
        parts = jnp.stack([mine, near, far, both])
        order = jnp.arange(SLOTS) ^ tensor
        return parts[order]

    section_out = spread_images(arrays[Y])
    input_grad = spread_images(arrays[DOWN]).astype(F32)
    qkv_grad = qkv_grad.astype(F32)
    rest = rest.astype(F32)
    head = rest[LANES:]
    outs = (
        section_out,
        input_grad,
        head[0:2],
        head[2:4],
        jnp.stack([qkv_grad[:, i * LANES : (i + 1) * LANES] for i in range(3)]),
        jnp.stack([head[7, 0:LANES], head[7, 2 * LANES : 3 * LANES]]),
        head[8:10].reshape(-1)[: REL * GROUP].reshape(REL, GROUP),
        rest[:LANES],
        head[4:6],
        fc1_grad.astype(F32),
        head[6],
        fc2_grad.astype(F32),
    )
    return tuple(out[None] for out in outs)


def solution(mesh):
    placed = (
        P(DP, None, None),
        P(DP, None, None),
        P(SEC, None, None),
        P(SEC, None, None),
        P(SEC, None, None, TEN),
        P(SEC, None, TEN),
        P(SEC, None, TEN),
        P(SEC, TEN, None),
        P(SEC, None, None),
        P(SEC, None, TEN),
        P(SEC, TEN),
        P(SEC, TEN, None),
        P(),
        P(),
    )
    return jax.shard_map(
        local,
        mesh=mesh,
        in_specs=placed,
        out_specs=(
            P(SEC, DP, None, None),
            P(SEC, DP, None, None),
            P(SEC, None, None),
            P(SEC, None, None),
            P(SEC, None, None, TEN),
            P(SEC, None, TEN),
            P(SEC, None, TEN),
            P(SEC, TEN, None),
            P(SEC, None, None),
            P(SEC, None, TEN),
            P(SEC, TEN),
            P(SEC, TEN, None),
        ),
        check_vma=False,
    )
```

```python
import functools

import jax
import jax.numpy as jnp
import numpy as np
from jax import lax
from jax.experimental import pallas as pl
from jax.experimental.pallas import tpu as pltpu
from jax.sharding import PartitionSpec as P

D = 512
HEAD_DIM = 32
WIN = 7
SIDE = 14
SHIFT = 3
PIX = 196
WTOK = 49
REL = 169
NWIN = 4

ROWS = 64
M = NWIN * ROWS
TOK = 208
GROUP = 4
LANES = GROUP * HEAD_DIM
WIDE = GROUP * ROWS
ATT_ROWS = 3 * D + D + 4 * 16 + 2 * ROWS
SLOTS = 4

EPS = 1e-05
SCALE = HEAD_DIM ** (-0.5)
BF = jnp.bfloat16
F32 = jnp.float32
HIGHEST = lax.Precision.HIGHEST

SEC, DP, TEN = "section", "dp", "tensor"

(
    X,
    TILES,
    XHAT1,
    R1,
    NORMED,
    BRANCH,
    MIDDLE,
    XHAT2,
    R2,
    NORMED2,
    RESULT,
    Y,
    GMLP,
    GMIDDLE,
    GBRANCH,
    SUMS_B,
    SUMS_C,
    SUMS_A,
    GTOTAL,
    DOWN,
    ARRIVED,
    UPSTREAM,
    IMAGE,
    PV,
    PERM,
    PERM_T,
    BIAS,
    REGION,
    WA,
    WB,
    QKV,
    PROBS,
    CTX,
    SLOPE,
    HIDDEN,
    GPRE,
    GQKV,
    SCORESUM,
    FC2G,
    FC1G,
    ATTG,
) = range(41)


def dot(a, b, ca, cb):
    return lax.dot_general(a, b, (((ca,), (cb,)), ((), ())), preferred_element_type=F32)


class Env:
    def __init__(self, refs, copies_in, copies_out):
        self.refs, self.copies_in, self.copies_out = refs, dict(copies_in), dict(copies_out)
        self.started = []

    def __getitem__(self, name):
        return self.refs[name]

    def need(self, name):
        for copy in self.copies_in.pop(name, ()):
            copy.wait()
        return self.refs[name]

    def emit(self, name):
        for copy in self.copies_out.pop(name, ()):
            copy.start()
            self.started.append(copy)

    def finish(self):
        for name in list(self.copies_in):
            self.need(name)
        for name in list(self.copies_out):
            self.emit(name)
        for copy in self.started:
            copy.wait()


def head_masks():
    lane = lax.broadcasted_iota(jnp.int32, (1, LANES), 1) // HEAD_DIM
    return [(lane == h).astype(F32) for h in range(GROUP)]


def spread(rows, masks):
    return jnp.concatenate([rows * mask.astype(BF) for mask in masks], axis=0)


def gather_heads(stacked, masks):
    total = stacked[0:ROWS] * masks[0]
    for h in range(1, GROUP):
        total = total + stacked[h * ROWS : (h + 1) * ROWS] * masks[h]
    return total


def norm_of(values):
    center = values - jnp.mean(values, -1, keepdims=True)
    r = lax.rsqrt(jnp.mean(center * center, -1, keepdims=True) + EPS)
    return center * r, r


def qkv_weight_of(ref):
    return jnp.concatenate([ref[i * D : (i + 1) * D] for i in range(3)], axis=1)


def proj_weight_of(ref):
    return jnp.concatenate(
        [ref[3 * D + i * LANES : 3 * D + (i + 1) * LANES] for i in range(D // LANES)], axis=1
    )


def image_norm(env):
    first_norm(env, dot(env[PERM][:, 0:PIX], env.need(IMAGE)[...], 1, 0))


def arrived_norm(env):
    first_norm(env, dot(env[PERM][...], env.need(X)[...], 1, 0))


def first_norm(env, tiles):
    xhat, r = norm_of(tiles)
    env[XHAT1][...] = xhat
    env.emit(XHAT1)
    env[R1][...] = jnp.broadcast_to(r, (M, 128))
    env.emit(R1)
    env[NORMED][...] = (xhat * env[PV][0:1, :] + env[PV][2:3, :]).astype(BF)
    env.emit(NORMED)
    env[BRANCH][...] = tiles + env[PV][4:5, :]


def forward_heads(env, slots):
    masks = head_masks()
    normed = env.need(NORMED)[...]
    branch = env.need(BRANCH)[...]
    regions = [jnp.concatenate([env[REGION][w]] * GROUP, axis=1) for w in range(NWIN)]
    empty = lax.broadcasted_iota(jnp.int32, (ROWS, WIDE), 0) >= WTOK
    for j in slots:
        weights = env.need((WA, j))
        bias = jnp.concatenate([env[BIAS][j * GROUP + h] for h in range(GROUP)], axis=1)
        bias = jnp.where(empty, -1e30, bias)
        packed = dot(normed, qkv_weight_of(weights), 1, 0) + env[PV][12 + j : 13 + j, 0 : 3 * LANES]
        packed = packed.astype(BF)
        env[QKV, j][...] = packed
        env.emit((QKV, j))
        parts = []
        for w in range(NWIN):
            rows = slice(w * ROWS, (w + 1) * ROWS)
            q = packed[rows, 0:LANES]
            k = packed[rows, LANES : 2 * LANES]
            v = packed[rows, 2 * LANES : 3 * LANES]
            scores = dot(k, spread(q, masks), 1, 1) * SCALE + bias + regions[w]
            exps = jnp.exp(scores - jnp.max(scores, 0, keepdims=True))
            probs = exps / jnp.sum(exps, 0, keepdims=True)
            env[PROBS, j][w] = probs
            parts.append(gather_heads(dot(probs.astype(BF), v, 0, 0), masks))
        env.emit((PROBS, j))
        context = jnp.concatenate(parts, axis=0).astype(BF)
        env[CTX, j][...] = context
        env.emit((CTX, j))
        branch = branch + dot(context, proj_weight_of(weights), 1, 0)
    return branch


def forward_near_heads(env):
    env[BRANCH][...] = forward_heads(env, (0, 1))
    env.emit(BRANCH)


def forward_far_heads(env):
    middle = forward_heads(env, (2, 3))
    xhat, r = norm_of(middle)
    env[XHAT2][...] = xhat
    env.emit(XHAT2)
    env[R2][...] = jnp.broadcast_to(r, (M, 128))
    env.emit(R2)
    env[NORMED2][...] = (xhat * env[PV][1:2, :] + env[PV][3:4, :]).astype(BF)
    env.emit(NORMED2)
    env[RESULT][...] = middle + env[PV][5:6, :]


def forward_hidden(env, slots):
    normed = env.need(NORMED2)[...]
    total = env.need(RESULT)[...]
    for j in slots:
        weights = env.need((WB, j))
        pre = dot(normed, weights[0:D], 1, 0) + env[PV][8 + j : 9 + j, :]
        phi = 0.5 * (1.0 + lax.erf(pre * (0.5**0.5)))
        hidden = (pre * phi).astype(BF)
        env[SLOPE, j][...] = phi + pre * jnp.exp(-0.5 * pre * pre) * (2.0 * np.pi) ** -0.5
        env.emit((SLOPE, j))
        env[HIDDEN, j][...] = hidden
        env.emit((HIDDEN, j))
        total = total + dot(hidden, weights[D : 2 * D], 1, 0)
    return total


def forward_near_hidden(env):
    env[RESULT][...] = forward_hidden(env, (0, 1))
    env.emit(RESULT)


def forward_far_hidden(env):
    total = forward_hidden(env, (2, 3))
    env[Y][...] = dot(env[PERM_T][...], total.astype(BF), 1, 0).astype(BF)
    env.emit(Y)


def backward_norm(grad, xhat, r, gain):
    u = grad * gain
    return r * (u - jnp.mean(u, -1, keepdims=True) - xhat * jnp.mean(u * xhat, -1, keepdims=True))


def column_sum(values):
    return jnp.sum(values, 0, keepdims=True)


def backward_mlp(env):
    gmlp = env[GMLP][...]
    gtiles = gmlp.astype(F32)
    sums = env[SUMS_B]
    sums[3:4, :] = column_sum(gtiles)
    total = jnp.zeros((M, D), F32)
    for j in range(SLOTS):
        weights = env.need((WB, j))
        gact = dot(gmlp, weights[D : 2 * D], 1, 1)
        gpre = (gact * env.need((SLOPE, j))[...]).astype(BF)
        env[GPRE, j][...] = gpre
        env.emit((GPRE, j))
        sums[4 + j : 5 + j, :] = column_sum(gpre.astype(F32))
        total = total + dot(gpre, weights[0:D], 1, 1)
    xhat = env.need(XHAT2)[...]
    r = env.need(R2)[:, 0:1]
    sums[0:1, :] = column_sum(total * xhat)
    sums[1:2, :] = column_sum(total)
    gmiddle = gtiles + backward_norm(total, xhat, r, env[PV][1:2, :])
    env[GMIDDLE][...] = gmiddle
    env.emit(GMIDDLE)
    gbranch = gmiddle.astype(BF)
    env[GBRANCH][...] = gbranch
    env.emit(GBRANCH)
    sums[2:3, :] = column_sum(gbranch.astype(F32))
    env.emit(SUMS_B)


def backward_heads(env, slots, total, sums):
    masks = head_masks()
    sums[...] = jnp.zeros_like(sums)
    gbranch = env.need(GBRANCH)[...]
    for j in slots:
        weights = env.need((WA, j))
        gcontext = dot(gbranch, proj_weight_of(weights), 1, 1).astype(BF)
        packed = env.need((QKV, j))[...]
        env.need((PROBS, j))
        score_sum = None
        parts = []
        for w in range(NWIN):
            rows = slice(w * ROWS, (w + 1) * ROWS)
            q = spread(packed[rows, 0:LANES], masks)
            k = packed[rows, LANES : 2 * LANES]
            v = packed[rows, 2 * LANES : 3 * LANES]
            up = spread(gcontext[rows], masks)
            probs = env[PROBS, j][w]
            gprobs = dot(v, up, 1, 1)
            gscores = probs * (gprobs - jnp.sum(gprobs * probs, 0, keepdims=True))
            low = gscores.astype(BF)
            wide = low.astype(F32)
            score_sum = wide if score_sum is None else score_sum + wide
            gv = dot(probs.astype(BF), up, 1, 0)
            gk = dot(low, q, 1, 0) * SCALE
            gq = gather_heads(dot(low, k, 0, 0), masks) * SCALE
            parts.append(jnp.concatenate([gq, gk, gv], axis=1).astype(BF))
        env[SCORESUM, j][...] = score_sum
        env.emit((SCORESUM, j))
        grads = jnp.concatenate(parts, axis=0)
        env[GQKV, j][...] = grads
        env.emit((GQKV, j))
        sums[4 + j : 5 + j, 0 : 3 * LANES] = column_sum(grads.astype(F32))
        total = total + dot(grads, qkv_weight_of(weights), 1, 1)
    return total


def backward_far_heads(env):
    env[GTOTAL][...] = backward_heads(env, (2, 3), jnp.zeros((M, D), F32), env[SUMS_C])
    env.emit(GTOTAL)
    env.emit(SUMS_C)


def backward_near_heads(env):
    sums = env[SUMS_A]
    total = backward_heads(env, (0, 1), env.need(GTOTAL)[...], sums)
    xhat = env.need(XHAT1)[...]
    r = env.need(R1)[:, 0:1]
    sums[0:1, :] = column_sum(total * xhat)
    sums[1:2, :] = column_sum(total)
    sums[2:4, :] = jnp.zeros((2, D), F32)
    env.emit(SUMS_A)
    down = env.need(GMIDDLE)[...] + backward_norm(total, xhat, r, env[PV][0:1, :])
    env[DOWN][...] = dot(env[PERM_T][...], down.astype(BF), 1, 0).astype(BF)
    env.emit(DOWN)


def own_gradient(env):
    env[GMLP][...] = dot(env[PERM][:, 0:PIX], env.need(UPSTREAM)[...], 1, 0).astype(BF)
    env.emit(GMLP)


def arrived_gradient(env):
    env[GMLP][...] = dot(env[PERM][...], env.need(ARRIVED)[...], 1, 0).astype(BF)
    env.emit(GMLP)


ORDER = (3, 1, 2, 0)


def fc2_gradient(env):
    gmlp = env[GMLP][...]
    for j in ORDER:
        env[FC2G, j][...] = dot(env.need((HIDDEN, j))[...], gmlp, 0, 0).astype(BF)
        env.emit((FC2G, j))


def fc1_gradient(env):
    normed = env.need(NORMED2)[...]
    for j in ORDER:
        env[FC1G, j][...] = dot(normed, env.need((GPRE, j))[...], 0, 0).astype(BF)
        env.emit((FC1G, j))


def attention_gradient(env, slots, sums_qv):
    normed = env.need(NORMED)[...]
    gbranch = env.need(GBRANCH)[...]
    sums_b = env.need(SUMS_B)[...]
    sums_qv = env.need(sums_qv)[...]
    for j in slots:
        target = env[ATTG, j]
        grads = dot(normed, env.need((GQKV, j))[...], 0, 0).astype(BF)
        for i in range(3):
            target[i * D : (i + 1) * D, :] = grads[:, i * LANES : (i + 1) * LANES]
        at = 3 * D
        proj = dot(env.need((CTX, j))[...], gbranch, 0, 0).astype(BF)
        small = [jnp.zeros((6, D), F32), sums_b[4 + j : 5 + j], sums_qv[4 + j : 5 + j]]
        small = jnp.concatenate(small + [jnp.zeros((8, D), F32)], axis=0).astype(BF)
        score = env.need((SCORESUM, j))[...].astype(BF)
        for block in (proj, small, score):
            for i in range(block.shape[1] // LANES):
                count = block.shape[0]
                target[at : at + count, :] = block[:, i * LANES : (i + 1) * LANES]
                at += count
        env.emit((ATTG, j))


def far_attention_gradient(env):
    attention_gradient(env, (3, 2), SUMS_C)


def near_attention_gradient(env):
    attention_gradient(env, (1, 0), SUMS_A)


def shapes_of():
    table = {}
    for name in (X, Y, DOWN, ARRIVED):
        table[name] = ((TOK, D), BF)
    for name in (IMAGE, UPSTREAM):
        table[name] = ((PIX, D), BF)
    for name in (NORMED, NORMED2, GMLP, GBRANCH):
        table[name] = ((M, D), BF)
    for name in (XHAT1, BRANCH, XHAT2, RESULT, GMIDDLE, GTOTAL):
        table[name] = ((M, D), F32)
    for name in (R1, R2):
        table[name] = ((M, 128), F32)
    for name in (SUMS_A, SUMS_B, SUMS_C):
        table[name] = ((8, D), F32)
    for j in range(SLOTS):
        table[WA, j] = ((4 * D, LANES), BF)
        table[WB, j] = ((2 * D, D), BF)
        table[QKV, j] = ((M, 3 * LANES), BF)
        table[PROBS, j] = ((NWIN, ROWS, WIDE), F32)
        table[CTX, j] = ((M, LANES), BF)
        table[SLOPE, j] = ((M, D), F32)
        table[HIDDEN, j] = ((M, D), BF)
        table[GPRE, j] = ((M, D), BF)
        table[GQKV, j] = ((M, 3 * LANES), BF)
        table[SCORESUM, j] = ((ROWS, WIDE), F32)
        table[FC2G, j] = ((D, D), BF)
        table[FC1G, j] = ((D, D), BF)
        table[ATTG, j] = ((ATT_ROWS, LANES), BF)
    return table


SHAPES = shapes_of()
PIECES = {(name, j): 2 for name in (FC2G, FC1G, ATTG) for j in (1, 3)}


def per_slot(*names, slots=range(SLOTS)):
    return [(name, j) for j in slots for name in names]


NEAR, FAR = (0, 1), (2, 3)


def union(lists):
    found = []
    for names in lists:
        found += [name for name in names if name not in found]
    return found


def run_stages(variants, place, small, arrays, keep=(), scratch=()):
    ins = union([variant[2] for variant in variants])
    outs = union([variant[3] for variant in variants])
    local = union([ins, outs, scratch])
    small_names = list(small)
    kept = [name for name in outs if name in keep]
    sources, operands = {}, []
    for name in ins:
        if name in kept:
            continue
        held = arrays[name] if isinstance(arrays[name], list) else [(arrays[name], None)]
        sources[name] = []
        for array, offset in held:
            sources[name].append((len(operands), offset))
            operands.append(array)
    targets, out_shapes = {}, []
    for name in outs:
        shape, dtype = SHAPES[name]
        count = PIECES.get(name, 1)
        targets[name] = list(range(len(out_shapes), len(out_shapes) + count))
        out_shapes += [jax.ShapeDtypeStruct((shape[0] // count,) + shape[1:], dtype)] * count
    n_small, n_in, n_out = len(small_names), len(operands), len(out_shapes)

    def kernel(*refs):
        where = refs[0]
        at = 1
        env_refs = dict(zip(small_names, refs[at : at + n_small]))
        at += n_small
        in_hbm = refs[at : at + n_in]
        at += n_in + len(kept)
        out_hbm = refs[at : at + n_out]
        at += n_out
        env_refs.update(zip(local, refs[at : at + len(local)]))
        sems = refs[at + len(local)]

        def rows_of(name, start, count):
            ref = env_refs[name]
            return ref if start is None else ref.at[pl.ds(start, count)]

        def run(stages, own_ins, own_outs):
            copies_in, copies_out = {}, {}
            for name in own_ins:
                copies_in[name] = []
                if name in kept:
                    held = out_hbm[targets[name][0]]
                    sem = sems.at[n_in + n_out + kept.index(name)]
                    copies_in[name].append(pltpu.make_async_copy(held, env_refs[name], sem))
                    copies_in[name][-1].start()
                    continue
                for i, offset in sources[name]:
                    source = in_hbm[i]
                    if name in (IMAGE, UPSTREAM):
                        source = source.at[where[2]]
                    count = source.shape[0]
                    start = None
                    if offset is not None:
                        start = pl.multiple_of(offset(where), count)
                    part = rows_of(name, start, count)
                    copies_in[name].append(pltpu.make_async_copy(source, part, sems.at[i]))
                    copies_in[name][-1].start()
            for name in own_outs:
                copies_out[name] = []
                for piece, i in enumerate(targets[name]):
                    count = out_hbm[i].shape[0]
                    start = piece * count if len(targets[name]) > 1 else None
                    part = rows_of(name, start, count)
                    copies_out[name].append(
                        pltpu.make_async_copy(part, out_hbm[i], sems.at[n_in + i])
                    )
            env = Env(env_refs, copies_in, copies_out)
            for stage in stages:
                stage(env)
            env.finish()

        for section, stages, own_ins, own_outs in variants:
            body = functools.partial(run, stages, own_ins, own_outs)
            if section is None:
                body()
            else:
                pl.when(where[0] == section)(body)

    vmem = pl.BlockSpec(memory_space=pltpu.VMEM)
    hbm = pl.BlockSpec(memory_space=pltpu.HBM)
    results = pl.pallas_call(
        kernel,
        out_shape=out_shapes,
        in_specs=[pl.BlockSpec(memory_space=pltpu.SMEM)]
        + [vmem] * n_small
        + [hbm] * (n_in + len(kept)),
        out_specs=[hbm] * n_out,
        scratch_shapes=[pltpu.VMEM(*SHAPES[name]) for name in local]
        + [pltpu.SemaphoreType.DMA((n_in + n_out + len(kept),))],
        input_output_aliases={
            1 + n_small + n_in + i: targets[name][0] for i, name in enumerate(kept)
        },
        compiler_params=pltpu.CompilerParams(vmem_limit_bytes=60 * 1024 * 1024),
        cost_estimate=pl.CostEstimate(flops=20_000_000_000, bytes_accessed=10_000, transcendentals=0),
    )(
        place,
        *[small[name] for name in small_names],
        *operands,
        *[arrays[name] for name in kept],
    )
    for name in outs:
        pieces = [results[i] for i in targets[name]]
        arrays[name] = pieces[0] if len(pieces) == 1 else pieces


def tile_places(shift):
    places = np.full((NWIN, ROWS), -1, np.int32)
    for w in range(NWIN):
        for r in range(WTOK):
            i = (w // 2) * WIN + r // WIN
            j = (w % 2) * WIN + r % WIN
            places[w, r] = ((i + shift) % SIDE) * SIDE + (j + shift) % SIDE
    return places.reshape(M)


def permutations(shifted):
    places = jnp.where(shifted, jnp.asarray(tile_places(SHIFT)), jnp.asarray(tile_places(0)))
    tokens = jnp.arange(TOK, dtype=jnp.int32)
    forth = (places[:, None] == tokens[None, :]).astype(BF)
    back = (tokens[:, None] == places[None, :]).astype(BF)
    return forth, back


def region_bias(regions, shifted):
    stripes = SIDE // WIN
    tiled = (
        regions.reshape(stripes, WIN, stripes, WIN)
        .transpose(0, 2, 1, 3)
        .reshape(stripes * stripes, WIN * WIN)
    )
    tiled = jnp.pad(tiled, ((0, 0), (0, ROWS - WTOK)))
    differ = (tiled[:, :, None] != tiled[:, None, :]) & shifted
    return jnp.where(differ, -100.0, 0.0).astype(F32)


def xor_permute(array, by):
    devices = lax.axis_size(TEN)
    return lax.ppermute(array, TEN, [(i, i ^ by) for i in range(devices)])


def gather_slots(array):
    across = xor_permute(array, 2)
    return [array, xor_permute(array, 1), across, xor_permute(across, 1)]


def section_permute(array, source):
    return lax.ppermute(array, SEC, [(source, 1 - source)])


def after(values, *others):
    count = len(values)
    return lax.optimization_barrier(tuple(values) + tuple(others))[:count]


def add_low(a, b):
    return (a.astype(F32) + b.astype(F32)).astype(BF)


class Pipeline:
    starts = (0.0, 11.0, 22.0)
    stages = (0.0, 10.5, 24.0, 34.0)

    def __init__(self):
        self.pieces, self.done, self.last = [], set(), ()
        self.halving = lax.axis_size(DP) == 4
        self.odd = lax.axis_index(DP) % 2 == 1

    def add(self, share, arriving):
        self.pieces.append((share, arriving))

    def events(self):
        found = [
            (self.starts[i] + self.stages[stage], i, stage)
            for i in range(len(self.pieces))
            for stage in range(4)
            if (i, stage) not in self.done
        ]
        return [(i, stage) for _, i, stage in sorted(found)]

    def tied(self, *values):
        return after(values, *self.last)

    def permuted(self, array, by):
        return lax.ppermute(array, DP, [(i, i ^ by) for i in range(4)])

    def advance(self, count):
        if not self.halving:
            return
        for i, stage in self.events()[:count]:
            mine, arriving = self.tied(*self.pieces[i])
            if stage == 0:
                total = add_low(mine, arriving)
                half = total.shape[0] // 2
                low, high = total[:half], total[half:]
                keep = jnp.where(self.odd, high, low)
                send = jnp.where(self.odd, low, high)
                self.last = (keep, send)
                state = (keep, self.permuted(send, 1))
            elif stage < 3:
                total = add_low(mine, arriving)
                self.last = (total,)
                state = (total, self.permuted(total, 3 - stage))
            else:
                low = jnp.where(self.odd, arriving, mine)
                high = jnp.where(self.odd, mine, arriving)
                state = jnp.concatenate([low, high])
                self.last = (arriving,)
            self.done.add((i, stage))
            self.pieces[i] = state

    def finish(self):
        if not self.halving:
            return [lax.psum(add_low(*piece), DP) for piece in self.pieces]
        self.advance(4 * len(self.pieces))
        return self.pieces


def local(
    images,
    out_grad,
    ln_gain,
    ln_bias,
    qkv_weight,
    qv_bias,
    pos_table,
    proj_weight,
    out_bias,
    fc1_weight,
    fc1_bias,
    fc2_weight,
    rel_index,
    regions,
):
    section = lax.axis_index(SEC)
    shifted = section == 1
    odd = lax.axis_index(DP) % 2
    tensor = lax.axis_index(TEN)
    place = jnp.stack([section, odd, tensor]).astype(jnp.int32)

    pad = jnp.zeros((LANES,), F32)
    row = jnp.concatenate([qv_bias[0, 0], pad, qv_bias[0, 1], pad])
    table = jnp.pad(pos_table[0].reshape(-1), (0, 2 * D - REL * GROUP)).reshape(2, D)
    own_small = jnp.concatenate([fc1_bias[0][None], row[None], table], axis=0)
    small_slots = gather_slots(own_small)
    arrays = {}
    proj = proj_weight[0]
    blocks = [qkv_weight[0, i] for i in range(3)]
    blocks += [proj[:, i * LANES : (i + 1) * LANES] for i in range(D // LANES)]
    packs = {WA: (jnp.concatenate(blocks), 1), WB: (jnp.concatenate([fc1_weight[0], fc2_weight[0]]), 2)}
    pairs = [(i, i ^ 1) for i in range(lax.axis_size(DP))]
    for name, (pack, count) in packs.items():
        arrays[name, 0] = pack
        arrays[name, 1] = xor_permute(pack, 1)
        arrays[name, 2], arrays[name, 3] = [], []
        half = pack.shape[0] // 2
        size = half // count
        for i in range(count):
            low, high = pack[i * size : (i + 1) * size], pack[half + i * size : half + (i + 1) * size]
            mine = xor_permute(jnp.where(odd == 1, high, low), 2)
            for array, flip in ((mine, 0), (lax.ppermute(mine, DP, pairs), 1)):

                def offset(where, flip=flip, i=i, half=half, size=size):
                    return (where[1] ^ flip) * half + i * size

                arrays[name, 2].append((array, offset))

    def forward_to_core(name, tie=None):
        parts = [array for array, _ in arrays[name, 2]]
        if tie is not None:
            parts[-1:] = after(parts[-1:], tie)
        offsets = [offset for _, offset in arrays[name, 2]]
        arrays[name, 3] = [(xor_permute(part, 1), at) for part, at in zip(parts, offsets)]

    forth, back = permutations(shifted)
    rel = jnp.pad(rel_index, ((0, ROWS - WTOK), (0, ROWS - WTOK)), constant_values=-1)
    onehot = (rel.T[None] == jnp.arange(REL, dtype=jnp.int32)[:, None, None]).astype(BF)
    onehot = onehot.reshape(REL, ROWS * ROWS)
    heads = jnp.stack([part[2:4].reshape(-1)[: REL * GROUP] for part in small_slots])
    heads = heads.reshape(SLOTS, REL, GROUP).transpose(0, 2, 1).reshape(SLOTS * GROUP, REL)
    top = heads.astype(BF)
    mid = (heads - top.astype(F32)).astype(BF)
    end = (heads - top.astype(F32) - mid.astype(F32)).astype(BF)
    bias = dot(jnp.concatenate([top, mid, end]), onehot, 1, 0).reshape(3, SLOTS * GROUP, -1)
    bias = (bias[0] + bias[1] + bias[2]).reshape(SLOTS * GROUP, ROWS, ROWS)
    region = region_bias(regions, shifted)
    vectors = jnp.concatenate(
        [ln_gain[0], ln_bias[0], out_bias[0], jnp.zeros((2, D), F32)]
        + [part[0:1] for part in small_slots]
        + [part[1:2] for part in small_slots],
        axis=0,
    )
    all_small = {PV: vectors, PERM: forth, PERM_T: back, BIAS: bias, REGION: region}

    def small(*names):
        return {name: all_small[name] for name in names}

    arrays[IMAGE] = [(images, None)]
    arrays[UPSTREAM] = [(out_grad, None)]
    run_stages(
        [(0, [image_norm, forward_near_heads], [IMAGE] + per_slot(WA, slots=NEAR),
          [XHAT1, R1, NORMED, BRANCH] + per_slot(QKV, PROBS, CTX, slots=NEAR))],
        place, small(PV, PERM, BIAS, REGION), arrays,
    )
    forward_to_core(WA, arrays[BRANCH])
    run_stages(
        [(0, [forward_far_heads, forward_near_hidden],
          [NORMED, BRANCH] + per_slot(WA, slots=FAR) + per_slot(WB, slots=NEAR),
          [XHAT2, R2, NORMED2, RESULT] + per_slot(QKV, PROBS, CTX, slots=FAR)
          + per_slot(SLOPE, HIDDEN, slots=NEAR))],
        place, small(PV, BIAS, REGION), arrays,
    )
    forward_to_core(WB, arrays[RESULT])
    run_stages(
        [(0, [forward_far_hidden], [NORMED2, RESULT] + per_slot(WB, slots=FAR),
          [Y] + per_slot(SLOPE, HIDDEN, slots=FAR))],
        place, small(PV, PERM_T), arrays,
    )
    arrays[X] = section_permute(arrays[Y], 0)
    kept = [NORMED, NORMED2, Y] + per_slot(CTX, HIDDEN)
    outs = kept + [GMLP, GBRANCH, SUMS_A, SUMS_B, SUMS_C, DOWN] + per_slot(GPRE, GQKV, SCORESUM)
    stages = [
        arrived_norm,
        forward_near_heads,
        forward_far_heads,
        forward_near_hidden,
        forward_far_hidden,
        own_gradient,
        backward_mlp,
        backward_far_heads,
        backward_near_heads,
    ]
    run_stages(
        [(1, stages, [X] + per_slot(WA) + per_slot(WB) + [UPSTREAM], outs)],
        place, small(PV, PERM, PERM_T, BIAS, REGION), arrays, keep=kept,
        scratch=[XHAT1, R1, BRANCH, XHAT2, R2, RESULT, GMIDDLE, GTOTAL]
        + per_slot(QKV, PROBS, SLOPE),
    )
    out_slots = gather_slots(arrays[Y])
    arrays[ARRIVED], out_slots = after((section_permute(arrays[DOWN], 1), tuple(out_slots)))
    fc2_out = [GMLP] + per_slot(FC2G)
    run_stages(
        [
            (0, [arrived_gradient, fc2_gradient], [ARRIVED] + per_slot(HIDDEN), fc2_out),
            (1, [own_gradient, fc2_gradient], [UPSTREAM] + per_slot(HIDDEN), fc2_out),
        ],
        place, small(PERM), arrays,
    )

    def to_partners(name):
        far = jnp.concatenate([xor_permute(piece, 1) for piece in arrays[name, 3]])
        own = jnp.concatenate([xor_permute(piece, 1) for piece in arrays[name, 1]])
        return add_low(arrays[name, 2], far), add_low(arrays[name, 0], own)

    fc2_far, fc2_own = to_partners(FC2G)
    gpre, grads = per_slot(GPRE), per_slot(FC1G)
    mlp_ins = [ARRIVED, XHAT2, R2, NORMED2] + per_slot(WB, SLOPE)
    run_stages(
        [
            (0, [arrived_gradient, backward_mlp, fc1_gradient], mlp_ins,
             gpre + [GMIDDLE, GBRANCH, SUMS_B] + grads),
            (1, [fc1_gradient], [NORMED2] + gpre, grads),
        ],
        place, small(PV, PERM), arrays, keep=gpre + [GBRANCH, SUMS_B], scratch=[GMLP],
    )
    (arrays[GBRANCH],) = after((arrays[GBRANCH],), fc2_far)
    fc1_far, fc1_own = to_partners(FC1G)
    far_state = per_slot(GQKV, SCORESUM, slots=FAR)
    near_state = per_slot(GQKV, SCORESUM, slots=NEAR)
    far_grads, near_grads = per_slot(ATTG, slots=FAR), per_slot(ATTG, slots=NEAR)
    far_given = [NORMED, GBRANCH, SUMS_B] + per_slot(CTX, slots=FAR)
    near_given = [NORMED, GBRANCH, SUMS_B] + per_slot(CTX, slots=NEAR)
    run_stages(
        [
            (0, [backward_far_heads, far_attention_gradient],
             far_given + per_slot(WA, QKV, PROBS, slots=FAR),
             far_state + [SUMS_C, GTOTAL] + far_grads),
            (1, [far_attention_gradient], far_given + far_state + [SUMS_C], far_grads),
        ],
        place, {}, arrays, keep=far_state + [SUMS_C],
    )
    pipeline = Pipeline()
    pipeline.last = (arrays[GTOTAL],)
    pipeline.add(fc2_own, xor_permute(fc2_far, 2))
    pipeline.advance(1)
    far = pipeline.tied(*arrays[ATTG, 3])
    att_far = add_low(arrays[ATTG, 2], jnp.concatenate([xor_permute(piece, 1) for piece in far]))
    pipeline.add(fc1_own, xor_permute(fc1_far, 2))
    pipeline.add(None, xor_permute(att_far, 2))
    arrays[GTOTAL], arrays[SUMS_B] = after((arrays[GTOTAL], arrays[SUMS_B]), fc1_far, att_far)
    run_stages(
        [
            (0, [backward_near_heads, near_attention_gradient],
             near_given + [GTOTAL, XHAT1, R1, GMIDDLE] + per_slot(WA, QKV, PROBS, slots=NEAR),
             near_state + [SUMS_A, DOWN] + near_grads),
            (1, [near_attention_gradient], near_given + near_state + [SUMS_A], near_grads),
        ],
        place, small(PV, PERM_T), arrays, keep=near_state + [SUMS_A, DOWN],
    )
    att_own = add_low(
        arrays[ATTG, 0], jnp.concatenate([xor_permute(piece, 1) for piece in arrays[ATTG, 1]])
    )
    sums_a, sums_b = arrays[SUMS_A], arrays[SUMS_B]
    shared = [sums_a[0:1], sums_b[0:1], sums_a[1:2], sums_b[1:2], sums_b[2:4]]
    shared = jnp.concatenate(shared + [jnp.zeros((10, D), F32)])
    shared = shared + xor_permute(shared, 1)
    shared = shared + xor_permute(shared, 2)
    shared = jnp.concatenate([shared[:, i * LANES : (i + 1) * LANES] for i in range(4)])
    at = 4 * D
    att_own = jnp.concatenate(
        [att_own[:at], (att_own[at : at + 64].astype(F32) + shared).astype(BF), att_own[at + 64 :]]
    )
    pipeline.last = (arrays[DOWN],)
    pipeline.pieces[2] = (att_own, pipeline.pieces[2][1])
    pipeline.advance(4)
    down_slots = gather_slots(pipeline.tied(arrays[DOWN])[0])
    sums = pipeline.finish()

    def spread_images(slots):
        odd, high = tensor % 2 == 1, tensor >= 2
        parts = [part[:PIX] for part in slots]
        pairs = []
        for a, b in (parts[0:2], parts[2:4]):
            pairs.append((jnp.where(odd, b, a), jnp.where(odd, a, b)))
        first = [jnp.where(high, b, a) for a, b in zip(*pairs)]
        second = [jnp.where(high, a, b) for a, b in zip(*pairs)]
        return jnp.stack(first + second)

    section_out = spread_images(out_slots)
    input_grad = spread_images(down_slots).astype(F32)
    fc2_grad, fc1_grad = sums[0].astype(F32), sums[1].astype(F32)
    qkv_grad = sums[2][: 3 * D].astype(F32).reshape(3, D, LANES)
    rest = sums[2][2 * D :]
    proj = rest[D : 2 * D].astype(F32).reshape(4, LANES, LANES)
    proj = jnp.concatenate([proj[i] for i in range(4)], axis=1)
    head = rest[2 * D : 2 * D + 64].astype(F32).reshape(4, 16, LANES)
    head = jnp.concatenate([head[i] for i in range(4)], axis=1)
    scores = rest[2 * D + 64 :].reshape(2, ROWS, 2, ROWS).transpose(0, 2, 1, 3)
    table_grad = dot(onehot, scores.reshape(GROUP, ROWS * ROWS), 1, 1)
    outs = (
        section_out,
        input_grad,
        head[0:2],
        head[2:4],
        qkv_grad,
        jnp.stack([head[7, 0:LANES], head[7, 2 * LANES : 3 * LANES]]),
        table_grad,
        proj,
        head[4:6],
        fc1_grad,
        head[6],
        fc2_grad,
    )
    return tuple(out[None] for out in outs)


def solution(mesh):
    placed = (
        P(DP, None, None),
        P(DP, None, None),
        P(SEC, None, None),
        P(SEC, None, None),
        P(SEC, None, None, TEN),
        P(SEC, None, TEN),
        P(SEC, None, TEN),
        P(SEC, TEN, None),
        P(SEC, None, None),
        P(SEC, None, TEN),
        P(SEC, TEN),
        P(SEC, TEN, None),
        P(),
        P(),
    )
    return jax.shard_map(
        local,
        mesh=mesh,
        in_specs=placed,
        out_specs=(
            P(SEC, DP, None, None),
            P(SEC, DP, None, None),
            P(SEC, None, None),
            P(SEC, None, None),
            P(SEC, None, None, TEN),
            P(SEC, None, TEN),
            P(SEC, None, TEN),
            P(SEC, TEN, None),
            P(SEC, None, None),
            P(SEC, None, TEN),
            P(SEC, TEN),
            P(SEC, TEN, None),
        ),
        check_vma=False,
    )
```

```python
import functools

import jax
import jax.numpy as jnp
import numpy as np
from jax import lax
from jax.experimental import pallas as pl
from jax.experimental.pallas import tpu as pltpu
from jax.sharding import PartitionSpec as P

D = 512
HEAD_DIM = 32
WIN = 7
SIDE = 14
SHIFT = 3
PIX = 196
WTOK = 49
REL = 169
NWIN = 4

ROWS = 64
M = NWIN * ROWS
TOK = 208
GROUP = 4
LANES = GROUP * HEAD_DIM
WIDE = GROUP * ROWS
ATT_SUMS = 3 * D + D + 4 * 16
ATT_ROWS = ATT_SUMS + 2 * ROWS
SLOTS = 4

EPS = 1e-05
SCALE = HEAD_DIM ** (-0.5)
BF = jnp.bfloat16
F32 = jnp.float32
HIGHEST = lax.Precision.HIGHEST

SEC, DP, TEN = "section", "dp", "tensor"

(
    X,
    TILES,
    XHAT1,
    R1,
    NORMED,
    BRANCH,
    MIDDLE,
    XHAT2,
    R2,
    NORMED2,
    RESULT,
    Y,
    GMLP,
    GMIDDLE,
    GBRANCH,
    SUMS_B,
    SUMS_C,
    SUMS_A,
    GTOTAL,
    DOWN,
    ARRIVED,
    UPSTREAM,
    IMAGE,
    PV,
    PERM,
    PERM_T,
    BIAS,
    REGION,
    WA,
    WB,
    QKV,
    PROBS,
    CTX,
    SLOPE,
    HIDDEN,
    GPRE,
    GQKV,
    SCORESUM,
    FC2G,
    FC1G,
    ATTG,
) = range(41)


def dot(a, b, ca, cb):
    return lax.dot_general(a, b, (((ca,), (cb,)), ((), ())), preferred_element_type=F32)


class Env:
    def __init__(self, refs, copies_in, copies_out):
        self.refs, self.copies_in, self.copies_out = refs, dict(copies_in), dict(copies_out)
        self.started = []

    def __getitem__(self, name):
        return self.refs[name]

    def need(self, name):
        for copy in self.copies_in.pop(name, ()):
            copy.wait()
        return self.refs[name]

    def emit(self, name):
        for copy in self.copies_out.pop(name, ()):
            copy.start()
            self.started.append(copy)

    def finish(self):
        for name in list(self.copies_in):
            self.need(name)
        for name in list(self.copies_out):
            self.emit(name)
        for copy in self.started:
            copy.wait()


def head_masks():
    lane = lax.broadcasted_iota(jnp.int32, (1, LANES), 1) // HEAD_DIM
    return [(lane == h).astype(F32) for h in range(GROUP)]


def spread(rows, masks):
    return jnp.concatenate([rows * mask.astype(BF) for mask in masks], axis=0)


def gather_heads(stacked, masks):
    total = stacked[0:ROWS] * masks[0]
    for h in range(1, GROUP):
        total = total + stacked[h * ROWS : (h + 1) * ROWS] * masks[h]
    return total


def norm_of(values):
    center = values - jnp.mean(values, -1, keepdims=True)
    r = lax.rsqrt(jnp.mean(center * center, -1, keepdims=True) + EPS)
    return center * r, r


def qkv_weight_of(ref):
    return jnp.concatenate([ref[i * D : (i + 1) * D] for i in range(3)], axis=1)


def proj_weight_of(ref):
    return jnp.concatenate(
        [ref[3 * D + i * LANES : 3 * D + (i + 1) * LANES] for i in range(D // LANES)], axis=1
    )


def image_norm(env):
    first_norm(env, dot(env[PERM][:, 0:PIX], env.need(IMAGE)[...], 1, 0))


def arrived_norm(env):
    first_norm(env, dot(env[PERM][...], env.need(X)[...], 1, 0))


def first_norm(env, tiles):
    xhat, r = norm_of(tiles)
    env[XHAT1][...] = xhat
    env.emit(XHAT1)
    env[R1][...] = jnp.broadcast_to(r, (M, 128))
    env.emit(R1)
    env[NORMED][...] = (xhat * env[PV][0:1, :] + env[PV][2:3, :]).astype(BF)
    env.emit(NORMED)
    env[BRANCH][...] = tiles + env[PV][4:5, :]


def forward_heads(env, slots):
    masks = head_masks()
    normed = env.need(NORMED)[...]
    branch = env.need(BRANCH)[...]
    regions = [jnp.concatenate([env[REGION][w]] * GROUP, axis=1) for w in range(NWIN)]
    empty = lax.broadcasted_iota(jnp.int32, (ROWS, WIDE), 0) >= WTOK
    for j in slots:
        weights = env.need((WA, j))
        bias = jnp.concatenate([env[BIAS][j * GROUP + h] for h in range(GROUP)], axis=1)
        bias = jnp.where(empty, -1e30, bias)
        packed = dot(normed, qkv_weight_of(weights), 1, 0) + env[PV][12 + j : 13 + j, 0 : 3 * LANES]
        packed = packed.astype(BF)
        env[QKV, j][...] = packed
        env.emit((QKV, j))
        parts = []
        for w in range(NWIN):
            rows = slice(w * ROWS, (w + 1) * ROWS)
            q = packed[rows, 0:LANES]
            k = packed[rows, LANES : 2 * LANES]
            v = packed[rows, 2 * LANES : 3 * LANES]
            scores = dot(k, spread(q, masks), 1, 1) * SCALE + bias + regions[w]
            exps = jnp.exp(scores - jnp.max(scores, 0, keepdims=True))
            probs = exps / jnp.sum(exps, 0, keepdims=True)
            env[PROBS, j][w] = probs
            parts.append(gather_heads(dot(probs.astype(BF), v, 0, 0), masks))
        env.emit((PROBS, j))
        context = jnp.concatenate(parts, axis=0).astype(BF)
        env[CTX, j][...] = context
        env.emit((CTX, j))
        branch = branch + dot(context, proj_weight_of(weights), 1, 0)
    return branch


def forward_near_heads(env):
    env[BRANCH][...] = forward_heads(env, (0, 1))
    env.emit(BRANCH)


def forward_far_heads(env):
    middle = forward_heads(env, (2, 3))
    xhat, r = norm_of(middle)
    env[XHAT2][...] = xhat
    env.emit(XHAT2)
    env[R2][...] = jnp.broadcast_to(r, (M, 128))
    env.emit(R2)
    env[NORMED2][...] = (xhat * env[PV][1:2, :] + env[PV][3:4, :]).astype(BF)
    env.emit(NORMED2)
    env[RESULT][...] = middle + env[PV][5:6, :]


def forward_hidden(env, slots):
    normed = env.need(NORMED2)[...]
    total = env.need(RESULT)[...]
    for j in slots:
        weights = env.need((WB, j))
        pre = dot(normed, weights[0:D], 1, 0) + env[PV][8 + j : 9 + j, :]
        phi = 0.5 * (1.0 + lax.erf(pre * (0.5**0.5)))
        hidden = (pre * phi).astype(BF)
        env[SLOPE, j][...] = phi + pre * jnp.exp(-0.5 * pre * pre) * (2.0 * np.pi) ** -0.5
        env.emit((SLOPE, j))
        env[HIDDEN, j][...] = hidden
        env.emit((HIDDEN, j))
        total = total + dot(hidden, weights[D : 2 * D], 1, 0)
    return total


def forward_near_hidden(env):
    env[RESULT][...] = forward_hidden(env, (0, 1))
    env.emit(RESULT)


def forward_far_hidden(env):
    total = forward_hidden(env, (2, 3))
    env[Y][...] = dot(env[PERM_T][...], total.astype(BF), 1, 0).astype(BF)
    env.emit(Y)


def backward_norm(grad, xhat, r, gain):
    u = grad * gain
    return r * (u - jnp.mean(u, -1, keepdims=True) - xhat * jnp.mean(u * xhat, -1, keepdims=True))


def column_sum(values):
    return jnp.sum(values, 0, keepdims=True)


def backward_mlp(env):
    gmlp = env[GMLP][...]
    gtiles = gmlp.astype(F32)
    sums = env[SUMS_B]
    sums[3:4, :] = column_sum(gtiles)
    total = jnp.zeros((M, D), F32)
    for j in range(SLOTS):
        weights = env.need((WB, j))
        gact = dot(gmlp, weights[D : 2 * D], 1, 1)
        gpre = (gact * env.need((SLOPE, j))[...]).astype(BF)
        env[GPRE, j][...] = gpre
        env.emit((GPRE, j))
        sums[4 + j : 5 + j, :] = column_sum(gpre.astype(F32))
        total = total + dot(gpre, weights[0:D], 1, 1)
    xhat = env.need(XHAT2)[...]
    r = env.need(R2)[:, 0:1]
    sums[0:1, :] = column_sum(total * xhat)
    sums[1:2, :] = column_sum(total)
    gmiddle = gtiles + backward_norm(total, xhat, r, env[PV][1:2, :])
    env[GMIDDLE][...] = gmiddle
    env.emit(GMIDDLE)
    gbranch = gmiddle.astype(BF)
    env[GBRANCH][...] = gbranch
    env.emit(GBRANCH)
    sums[2:3, :] = column_sum(gbranch.astype(F32))
    env.emit(SUMS_B)


def backward_heads(env, slots, total, sums):
    masks = head_masks()
    sums[...] = jnp.zeros_like(sums)
    gbranch = env.need(GBRANCH)[...]
    for j in slots:
        weights = env.need((WA, j))
        gcontext = dot(gbranch, proj_weight_of(weights), 1, 1).astype(BF)
        packed = env.need((QKV, j))[...]
        env.need((PROBS, j))
        score_sum = None
        parts = []
        for w in range(NWIN):
            rows = slice(w * ROWS, (w + 1) * ROWS)
            q = spread(packed[rows, 0:LANES], masks)
            k = packed[rows, LANES : 2 * LANES]
            v = packed[rows, 2 * LANES : 3 * LANES]
            up = spread(gcontext[rows], masks)
            probs = env[PROBS, j][w]
            gprobs = dot(v, up, 1, 1)
            gscores = probs * (gprobs - jnp.sum(gprobs * probs, 0, keepdims=True))
            low = gscores.astype(BF)
            wide = low.astype(F32)
            score_sum = wide if score_sum is None else score_sum + wide
            gv = dot(probs.astype(BF), up, 1, 0)
            gk = dot(low, q, 1, 0) * SCALE
            gq = gather_heads(dot(low, k, 0, 0), masks) * SCALE
            parts.append(jnp.concatenate([gq, gk, gv], axis=1).astype(BF))
        env[SCORESUM, j][...] = score_sum
        env.emit((SCORESUM, j))
        grads = jnp.concatenate(parts, axis=0)
        env[GQKV, j][...] = grads
        env.emit((GQKV, j))
        sums[4 + j : 5 + j, 0 : 3 * LANES] = column_sum(grads.astype(F32))
        total = total + dot(grads, qkv_weight_of(weights), 1, 1)
    return total


def backward_far_heads(env):
    env[GTOTAL][...] = backward_heads(env, (2, 3), jnp.zeros((M, D), F32), env[SUMS_C])
    env.emit(GTOTAL)
    env.emit(SUMS_C)


def backward_near_heads(env):
    sums = env[SUMS_A]
    total = backward_heads(env, (0, 1), env.need(GTOTAL)[...], sums)
    xhat = env.need(XHAT1)[...]
    r = env.need(R1)[:, 0:1]
    sums[0:1, :] = column_sum(total * xhat)
    sums[1:2, :] = column_sum(total)
    sums[2:4, :] = jnp.zeros((2, D), F32)
    env.emit(SUMS_A)
    down = env.need(GMIDDLE)[...] + backward_norm(total, xhat, r, env[PV][0:1, :])
    env[DOWN][...] = dot(env[PERM_T][...], down.astype(BF), 1, 0).astype(BF)
    env.emit(DOWN)


def own_gradient(env):
    env[GMLP][...] = dot(env[PERM][:, 0:PIX], env.need(UPSTREAM)[...], 1, 0).astype(BF)
    env.emit(GMLP)


def arrived_gradient(env):
    env[GMLP][...] = dot(env[PERM][...], env.need(ARRIVED)[...], 1, 0).astype(BF)
    env.emit(GMLP)


ORDER = (3, 1, 2, 0)


def fc2_gradient(env):
    gmlp = env[GMLP][...]
    for j in ORDER:
        env[FC2G, j][...] = dot(env.need((HIDDEN, j))[...], gmlp, 0, 0).astype(BF)
        env.emit((FC2G, j))


def fc1_gradient(env):
    normed = env.need(NORMED2)[...]
    for j in ORDER:
        env[FC1G, j][...] = dot(normed, env.need((GPRE, j))[...], 0, 0).astype(BF)
        env.emit((FC1G, j))


def attention_gradient(env, slots, sums_qv):
    normed = env.need(NORMED)[...]
    gbranch = env.need(GBRANCH)[...]
    sums_b = env.need(SUMS_B)[...]
    sums_qv = env.need(sums_qv)[...]
    for j in slots:
        target = env[ATTG, j]
        grads = dot(normed, env.need((GQKV, j))[...], 0, 0).astype(BF)
        for i in range(3):
            target[i * D : (i + 1) * D, :] = grads[:, i * LANES : (i + 1) * LANES]
        at = 3 * D
        proj = dot(env.need((CTX, j))[...], gbranch, 0, 0).astype(BF)
        small = [jnp.zeros((6, D), F32), sums_b[4 + j : 5 + j], sums_qv[4 + j : 5 + j]]
        small = jnp.concatenate(small + [jnp.zeros((8, D), F32)], axis=0).astype(BF)
        for block in (proj, small, env.need((SCORESUM, j))[...].astype(BF)):
            for i in range(block.shape[1] // LANES):
                count = block.shape[0]
                target[at : at + count, :] = block[:, i * LANES : (i + 1) * LANES]
                at += count
        env.emit((ATTG, j))


def far_attention_gradient(env):
    attention_gradient(env, (3, 2), SUMS_C)


def near_attention_gradient(env):
    attention_gradient(env, (1, 0), SUMS_A)


def shapes_of():
    table = {}
    for name in (X, Y, DOWN, ARRIVED):
        table[name] = ((TOK, D), BF)
    for name in (IMAGE, UPSTREAM):
        table[name] = ((PIX, D), BF)
    for name in (NORMED, NORMED2, GMLP, GBRANCH):
        table[name] = ((M, D), BF)
    for name in (XHAT1, BRANCH, XHAT2, RESULT, GMIDDLE, GTOTAL):
        table[name] = ((M, D), F32)
    for name in (R1, R2):
        table[name] = ((M, 128), F32)
    for name in (SUMS_A, SUMS_B, SUMS_C):
        table[name] = ((8, D), F32)
    for j in range(SLOTS):
        table[WA, j] = ((4 * D, LANES), BF)
        table[WB, j] = ((2 * D, D), BF)
        table[QKV, j] = ((M, 3 * LANES), BF)
        table[PROBS, j] = ((NWIN, ROWS, WIDE), F32)
        table[CTX, j] = ((M, LANES), BF)
        table[SLOPE, j] = ((M, D), F32)
        table[HIDDEN, j] = ((M, D), BF)
        table[GPRE, j] = ((M, D), BF)
        table[GQKV, j] = ((M, 3 * LANES), BF)
        table[SCORESUM, j] = ((ROWS, WIDE), F32)
        table[FC2G, j] = ((D, D), BF)
        table[FC1G, j] = ((D, D), BF)
        table[ATTG, j] = ((ATT_ROWS, LANES), BF)
    return table


SHAPES = shapes_of()
PIECES = {(name, j): 2 for name in (FC2G, FC1G, ATTG) for j in (1, 3)}


def per_slot(*names, slots=range(SLOTS)):
    return [(name, j) for j in slots for name in names]


NEAR, FAR = (0, 1), (2, 3)


def union(lists):
    found = []
    for names in lists:
        found += [name for name in names if name not in found]
    return found


def run_stages(variants, place, small, arrays, keep=(), scratch=()):
    ins = union([variant[2] for variant in variants])
    outs = union([variant[3] for variant in variants])
    local = union([ins, outs, scratch])
    small_names = list(small)
    kept = [name for name in outs if name in keep]
    sources, operands = {}, []
    for name in ins:
        if name in kept:
            continue
        held = arrays[name] if isinstance(arrays[name], list) else [(arrays[name], None)]
        sources[name] = []
        for array, offset in held:
            sources[name].append((len(operands), offset))
            operands.append(array)
    targets, out_shapes = {}, []
    for name in outs:
        shape, dtype = SHAPES[name]
        count = PIECES.get(name, 1)
        targets[name] = list(range(len(out_shapes), len(out_shapes) + count))
        out_shapes += [jax.ShapeDtypeStruct((shape[0] // count,) + shape[1:], dtype)] * count
    n_small, n_in, n_out = len(small_names), len(operands), len(out_shapes)

    def kernel(*refs):
        where = refs[0]
        at = 1
        env_refs = dict(zip(small_names, refs[at : at + n_small]))
        at += n_small
        in_hbm = refs[at : at + n_in]
        at += n_in + len(kept)
        out_hbm = refs[at : at + n_out]
        at += n_out
        env_refs.update(zip(local, refs[at : at + len(local)]))
        sems = refs[at + len(local)]

        def rows_of(name, start, count):
            ref = env_refs[name]
            return ref if start is None else ref.at[pl.ds(start, count)]

        def run(stages, own_ins, own_outs):
            copies_in, copies_out = {}, {}
            for name in own_ins:
                copies_in[name] = []
                if name in kept:
                    held = out_hbm[targets[name][0]]
                    sem = sems.at[n_in + n_out + kept.index(name)]
                    copies_in[name].append(pltpu.make_async_copy(held, env_refs[name], sem))
                    copies_in[name][-1].start()
                    continue
                for i, offset in sources[name]:
                    source = in_hbm[i]
                    if name in (IMAGE, UPSTREAM):
                        source = source.at[where[2]]
                    count = source.shape[0]
                    start = None
                    if callable(offset):
                        start = pl.multiple_of(offset(where), count)
                    elif offset is not None:
                        start = offset
                    part = rows_of(name, start, count)
                    copies_in[name].append(pltpu.make_async_copy(source, part, sems.at[i]))
                    copies_in[name][-1].start()
            for name in own_outs:
                copies_out[name] = []
                for piece, i in enumerate(targets[name]):
                    count = out_hbm[i].shape[0]
                    start = piece * count if len(targets[name]) > 1 else None
                    part = rows_of(name, start, count)
                    copies_out[name].append(
                        pltpu.make_async_copy(part, out_hbm[i], sems.at[n_in + i])
                    )
            env = Env(env_refs, copies_in, copies_out)
            for stage in stages:
                stage(env)
            env.finish()

        for section, stages, own_ins, own_outs in variants:
            body = functools.partial(run, stages, own_ins, own_outs)
            if section is None:
                body()
            else:
                pl.when(where[0] == section)(body)

    vmem = pl.BlockSpec(memory_space=pltpu.VMEM)
    hbm = pl.BlockSpec(memory_space=pltpu.HBM)
    results = pl.pallas_call(
        kernel,
        out_shape=out_shapes,
        in_specs=[pl.BlockSpec(memory_space=pltpu.SMEM)]
        + [vmem] * n_small
        + [hbm] * (n_in + len(kept)),
        out_specs=[hbm] * n_out,
        scratch_shapes=[pltpu.VMEM(*SHAPES[name]) for name in local]
        + [pltpu.SemaphoreType.DMA((n_in + n_out + len(kept),))],
        input_output_aliases={
            1 + n_small + n_in + i: targets[name][0] for i, name in enumerate(kept)
        },
        compiler_params=pltpu.CompilerParams(vmem_limit_bytes=60 * 1024 * 1024),
        cost_estimate=pl.CostEstimate(flops=20_000_000_000, bytes_accessed=10_000, transcendentals=0),
    )(
        place,
        *[small[name] for name in small_names],
        *operands,
        *[arrays[name] for name in kept],
    )
    for name in outs:
        pieces = [results[i] for i in targets[name]]
        arrays[name] = pieces[0] if len(pieces) == 1 else pieces


def attention_outputs(swapped, rel, mine, arriving):
    def kernel(swap, rel, mine, arriving, *refs):
        qkv, proj, gains, shifts, biases, fc1_row, qv_rows, table, bins = refs
        flip = swap[0] == 1
        a, b = mine[...].astype(F32), arriving[...].astype(F32)
        rows = jnp.concatenate([jnp.where(flip, b, a), jnp.where(flip, a, b)], axis=0)
        qkv[...] = rows[: 3 * D]
        for i in range(4):
            lanes = slice(i * LANES, (i + 1) * LANES)
            proj[:, lanes] = rows[3 * D + i * LANES : 3 * D + (i + 1) * LANES]
            small = rows[4 * D + 16 * i : 4 * D + 16 * (i + 1)]
            gains[:, lanes] = small[0:2]
            shifts[:, lanes] = small[2:4]
            biases[:, lanes] = small[4:6]
            fc1_row[:, lanes] = small[6:7]
            if i in (0, 2):
                qv_rows[i // 2 : i // 2 + 1, :] = small[7:8]
        scores = [rows[ATT_SUMS : ATT_SUMS + ROWS], rows[ATT_SUMS + ROWS :]]
        scores = jnp.concatenate(scores, axis=1)
        where = rel[...]

        def eight(i, carry):
            found = [column_sum(jnp.where(where == i * 8 + r, scores, 0.0)) for r in range(8)]
            bins[pl.ds(pl.multiple_of(i * 8, 8), 8), :] = jnp.concatenate(found, axis=0)
            return carry

        bins[...] = jnp.zeros_like(bins)
        lax.fori_loop(0, (REL + 7) // 8, eight, 0)
        head = lax.broadcasted_iota(jnp.int32, (LANES, WIDE), 0)
        pick = (head == lax.broadcasted_iota(jnp.int32, (LANES, WIDE), 1) // ROWS).astype(BF)
        sums = bins[...]
        high = sums.astype(BF)
        sums = dot(high, pick, 1, 1) + dot((sums - high.astype(F32)).astype(BF), pick, 1, 1)
        table[...] = sums[:REL, :GROUP]

    shapes = [(3 * D, LANES), (LANES, D), (2, D), (2, D), (2, D), (1, D), (2, LANES), (REL, GROUP)]
    vmem = pl.BlockSpec(memory_space=pltpu.VMEM)
    return pl.pallas_call(
        kernel,
        out_shape=[jax.ShapeDtypeStruct(shape, F32) for shape in shapes],
        in_specs=[pl.BlockSpec(memory_space=pltpu.SMEM)] + [vmem] * 3,
        out_specs=[vmem] * len(shapes),
        scratch_shapes=[pltpu.VMEM((2 * LANES, WIDE), F32)],
        compiler_params=pltpu.CompilerParams(vmem_limit_bytes=32 * 1024 * 1024),
    )(swapped, rel, mine, arriving)


def tile_places(shift):
    places = np.full((NWIN, ROWS), -1, np.int32)
    for w in range(NWIN):
        for r in range(WTOK):
            i = (w // 2) * WIN + r // WIN
            j = (w % 2) * WIN + r % WIN
            places[w, r] = ((i + shift) % SIDE) * SIDE + (j + shift) % SIDE
    return places.reshape(M)


def permutations(shifted):
    places = jnp.where(shifted, jnp.asarray(tile_places(SHIFT)), jnp.asarray(tile_places(0)))
    tokens = jnp.arange(TOK, dtype=jnp.int32)
    forth = (places[:, None] == tokens[None, :]).astype(BF)
    back = (tokens[:, None] == places[None, :]).astype(BF)
    return forth, back


def region_bias(regions, shifted):
    stripes = SIDE // WIN
    tiled = (
        regions.reshape(stripes, WIN, stripes, WIN)
        .transpose(0, 2, 1, 3)
        .reshape(stripes * stripes, WIN * WIN)
    )
    tiled = jnp.pad(tiled, ((0, 0), (0, ROWS - WTOK)))
    differ = (tiled[:, :, None] != tiled[:, None, :]) & shifted
    return jnp.where(differ, -100.0, 0.0).astype(F32)


def xor_permute(array, by):
    devices = lax.axis_size(TEN)
    return lax.ppermute(array, TEN, [(i, i ^ by) for i in range(devices)])


def gather_slots(array):
    across = xor_permute(array, 2)
    return [array, xor_permute(array, 1), across, xor_permute(across, 1)]


def section_permute(array, source):
    return lax.ppermute(array, SEC, [(source, 1 - source)])


def after(values, *others):
    count = len(values)
    return lax.optimization_barrier(tuple(values) + tuple(others))[:count]


def add_low(a, b):
    return (a.astype(F32) + b.astype(F32)).astype(BF)


class Pipeline:
    order = (
        (0, 0), (0, 1), (1, 0), (1, 1), (2, 0), (0, 2),
        (2, 1), (0, 3), (1, 2), (2, 2), (1, 3), (2, 3),
    )

    def __init__(self):
        self.pieces, self.done, self.last = [], set(), ()
        self.halving = lax.axis_size(DP) == 4
        self.odd = lax.axis_index(DP) % 2 == 1

    def add(self, share, arriving):
        self.pieces.append((share, arriving))

    def events(self):
        return [event for event in self.order if event not in self.done]

    def tied(self, *values):
        return after(values, *self.last)

    def permuted(self, array, by):
        return lax.ppermute(array, DP, [(i, i ^ by) for i in range(4)])

    def advance(self, count):
        if not self.halving:
            return
        for i, stage in self.events()[:count]:
            mine, arriving = self.tied(*self.pieces[i])
            if stage == 0:
                total = add_low(mine, arriving)
                half = total.shape[0] // 2
                low, high = total[:half], total[half:]
                keep = jnp.where(self.odd, high, low)
                send = jnp.where(self.odd, low, high)
                self.last = (keep, send)
                state = (keep, self.permuted(send, 1))
            elif stage < 3:
                total = add_low(mine, arriving)
                self.last = (total,)
                state = (total, self.permuted(total, 3 - stage))
            elif i == 2:
                state = (mine, arriving)
            else:
                low = jnp.where(self.odd, arriving, mine)
                high = jnp.where(self.odd, mine, arriving)
                state = jnp.concatenate([low, high])
                self.last = (arriving,)
            self.done.add((i, stage))
            self.pieces[i] = state

    def finish(self):
        if not self.halving:
            sums = [lax.psum(add_low(*piece), DP) for piece in self.pieces]
            return sums[:2] + [jnp.split(sums[2], 2)]
        self.advance(4 * len(self.pieces))
        return self.pieces


def local(
    images,
    out_grad,
    ln_gain,
    ln_bias,
    qkv_weight,
    qv_bias,
    pos_table,
    proj_weight,
    out_bias,
    fc1_weight,
    fc1_bias,
    fc2_weight,
    rel_index,
    regions,
):
    section = lax.axis_index(SEC)
    shifted = section == 1
    odd = lax.axis_index(DP) % 2
    tensor = lax.axis_index(TEN)
    place = jnp.stack([section, odd, tensor]).astype(jnp.int32)

    arrays = {}
    qkv = qkv_weight[0].reshape(3 * D, LANES)
    proj = proj_weight[0]
    proj = jnp.concatenate([proj[:, i * LANES : (i + 1) * LANES] for i in range(D // LANES)])
    fc1, fc2 = fc1_weight[0], fc2_weight[0]
    quarter = D // 2
    first = jnp.where(odd == 1, jnp.concatenate([qkv[2 * D :], proj]), qkv[: 2 * D])
    chosen = {WA: [first], WB: []}
    for i in range(2):
        rows = slice(i * quarter, (i + 1) * quarter)
        chosen[WB].append(jnp.where(odd == 1, fc2[rows], fc1[rows]))
    arrays[WA, 0] = [(qkv, 0), (proj, 3 * D)]
    arrays[WB, 0] = [(fc1, 0), (fc2, D)]
    pairs = [(i, i ^ 1) for i in range(lax.axis_size(DP))]
    for name, half in ((WA, 2 * D), (WB, D)):
        arrays[name, 1] = [(xor_permute(array, 1), at) for array, at in arrays[name, 0]]
        arrays[name, 2] = []
        for i, part in enumerate(chosen[name]):
            mine = xor_permute(part, 2)
            for array, flip in ((mine, 0), (lax.ppermute(mine, DP, pairs), 1)):

                def offset(where, flip=flip, half=half, start=i * quarter):
                    return (where[1] ^ flip) * half + start

                arrays[name, 2].append((array, offset))

    pad = jnp.zeros((LANES,), F32)
    fc1_bias, qv_bias, pos_table = after((fc1_bias, qv_bias, pos_table), first, *chosen[WB])
    row = jnp.concatenate([qv_bias[0, 0], pad, qv_bias[0, 1], pad])
    table = jnp.pad(pos_table[0].reshape(-1), (0, 2 * D - REL * GROUP)).reshape(2, D)
    own_small = jnp.concatenate([fc1_bias[0][None], row[None], table], axis=0)
    small_slots = gather_slots(own_small)

    def forward_to_core(name, tie=None):
        parts = [array for array, _ in arrays[name, 2]]
        if tie is not None:
            parts[1::2] = after(parts[1::2], tie)
        offsets = [offset for _, offset in arrays[name, 2]]
        arrays[name, 3] = [(xor_permute(part, 1), at) for part, at in zip(parts, offsets)]

    forth, back = permutations(shifted)
    rel = jnp.pad(rel_index, ((0, ROWS - WTOK), (0, ROWS - WTOK)), constant_values=-1)
    onehot = (rel.T[None] == jnp.arange(REL, dtype=jnp.int32)[:, None, None]).astype(BF)
    onehot = onehot.reshape(REL, ROWS * ROWS)
    heads = jnp.stack([part[2:4].reshape(-1)[: REL * GROUP] for part in small_slots])
    heads = heads.reshape(SLOTS, REL, GROUP).transpose(0, 2, 1).reshape(SLOTS * GROUP, REL)
    top = heads.astype(BF)
    mid = (heads - top.astype(F32)).astype(BF)
    end = (heads - top.astype(F32) - mid.astype(F32)).astype(BF)
    bias = dot(jnp.concatenate([top, mid, end]), onehot, 1, 0).reshape(3, SLOTS * GROUP, -1)
    bias = (bias[0] + bias[1] + bias[2]).reshape(SLOTS * GROUP, ROWS, ROWS)
    region = region_bias(regions, shifted)
    vectors = jnp.concatenate(
        [ln_gain[0], ln_bias[0], out_bias[0], jnp.zeros((2, D), F32)]
        + [part[0:1] for part in small_slots]
        + [part[1:2] for part in small_slots],
        axis=0,
    )
    all_small = {PV: vectors, PERM: forth, PERM_T: back, BIAS: bias, REGION: region}
    rel_wide = jnp.tile(rel.T, (1, GROUP))

    def small(*names):
        return {name: all_small[name] for name in names}

    arrays[IMAGE] = [(images, None)]
    arrays[UPSTREAM] = [(out_grad, None)]
    run_stages(
        [(0, [image_norm, forward_near_heads], [IMAGE] + per_slot(WA, slots=NEAR),
          [XHAT1, R1, NORMED, BRANCH] + per_slot(QKV, PROBS, CTX, slots=NEAR))],
        place, small(PV, PERM, BIAS, REGION), arrays,
    )
    forward_to_core(WA, arrays[BRANCH])
    run_stages(
        [(0, [forward_far_heads, forward_near_hidden],
          [NORMED, BRANCH] + per_slot(WA, slots=FAR) + per_slot(WB, slots=NEAR),
          [XHAT2, R2, NORMED2, RESULT] + per_slot(QKV, PROBS, CTX, slots=FAR)
          + per_slot(SLOPE, HIDDEN, slots=NEAR))],
        place, small(PV, BIAS, REGION), arrays,
    )
    forward_to_core(WB, arrays[RESULT])
    run_stages(
        [(0, [forward_far_hidden], [NORMED2, RESULT] + per_slot(WB, slots=FAR),
          [Y] + per_slot(SLOPE, HIDDEN, slots=FAR))],
        place, small(PV, PERM_T), arrays,
    )
    arrays[X] = section_permute(arrays[Y], 0)
    kept = [NORMED, NORMED2, Y] + per_slot(CTX, HIDDEN)
    outs = kept + [GMLP, GBRANCH, SUMS_A, SUMS_B, SUMS_C, DOWN] + per_slot(GPRE, GQKV, SCORESUM)
    stages = [
        arrived_norm,
        forward_near_heads,
        forward_far_heads,
        forward_near_hidden,
        forward_far_hidden,
        own_gradient,
        backward_mlp,
        backward_far_heads,
        backward_near_heads,
    ]
    run_stages(
        [(1, stages, [X] + per_slot(WA) + per_slot(WB) + [UPSTREAM], outs)],
        place, small(PV, PERM, PERM_T, BIAS, REGION), arrays, keep=kept,
        scratch=[XHAT1, R1, BRANCH, XHAT2, R2, RESULT, GMIDDLE, GTOTAL]
        + per_slot(QKV, PROBS, SLOPE),
    )
    out_slots = gather_slots(arrays[Y])
    arrays[ARRIVED], out_slots = after((section_permute(arrays[DOWN], 1), tuple(out_slots)))
    fc2_out = [GMLP] + per_slot(FC2G)
    run_stages(
        [
            (0, [arrived_gradient, fc2_gradient], [ARRIVED] + per_slot(HIDDEN), fc2_out),
            (1, [own_gradient, fc2_gradient], [UPSTREAM] + per_slot(HIDDEN), fc2_out),
        ],
        place, small(PERM), arrays,
    )

    def to_partners(name):
        far = jnp.concatenate([xor_permute(piece, 1) for piece in arrays[name, 3]])
        own = jnp.concatenate([xor_permute(piece, 1) for piece in arrays[name, 1]])
        return add_low(arrays[name, 2], far), add_low(arrays[name, 0], own)

    fc2_far, fc2_own = to_partners(FC2G)
    gpre, grads = per_slot(GPRE), per_slot(FC1G)
    far_state = per_slot(GQKV, SCORESUM, slots=FAR)
    near_state = per_slot(GQKV, SCORESUM, slots=NEAR)
    far_grads, near_grads = per_slot(ATTG, slots=FAR), per_slot(ATTG, slots=NEAR)
    (arrays[ARRIVED],) = after((arrays[ARRIVED],), fc2_far)
    run_stages(
        [
            (0, [arrived_gradient, backward_mlp, fc1_gradient, backward_far_heads, far_attention_gradient],
             [ARRIVED, XHAT2, R2, NORMED2] + per_slot(WB, SLOPE)
             + per_slot(WA, QKV, PROBS, CTX, slots=FAR) + [NORMED],
             gpre + [GMIDDLE, GBRANCH, SUMS_B] + grads + far_state + [SUMS_C, GTOTAL] + far_grads),
            (1, [fc1_gradient, far_attention_gradient],
             [NORMED2] + gpre + [NORMED, GBRANCH, SUMS_B] + per_slot(CTX, slots=FAR)
             + far_state + [SUMS_C],
             grads + far_grads),
        ],
        place, small(PV, PERM), arrays, keep=gpre + [GBRANCH, SUMS_B, SUMS_C] + far_state,
        scratch=[GMLP],
    )
    near_given = [NORMED, GBRANCH, SUMS_B] + per_slot(CTX, slots=NEAR)
    fc1_far, fc1_own = to_partners(FC1G)
    pipeline = Pipeline()
    pipeline.last = (arrays[GTOTAL],)
    pipeline.add(fc2_own, xor_permute(fc2_far, 2))
    pipeline.advance(1)
    far = pipeline.tied(*arrays[ATTG, 3])
    att_far = add_low(arrays[ATTG, 2], jnp.concatenate([xor_permute(piece, 1) for piece in far]))
    pipeline.add(fc1_own, xor_permute(fc1_far, 2))
    pipeline.add(None, xor_permute(att_far, 2))
    arrays[GTOTAL], arrays[SUMS_B] = after((arrays[GTOTAL], arrays[SUMS_B]), fc1_far, att_far)
    run_stages(
        [
            (0, [backward_near_heads, near_attention_gradient],
             near_given + [GTOTAL, XHAT1, R1, GMIDDLE] + per_slot(WA, QKV, PROBS, slots=NEAR),
             near_state + [SUMS_A, DOWN] + near_grads),
            (1, [near_attention_gradient], near_given + near_state + [SUMS_A], near_grads),
        ],
        place, small(PV, PERM_T), arrays, keep=near_state + [SUMS_A, DOWN],
    )
    att_own = add_low(
        arrays[ATTG, 0], jnp.concatenate([xor_permute(piece, 1) for piece in arrays[ATTG, 1]])
    )
    sums_a, sums_b = arrays[SUMS_A], arrays[SUMS_B]
    shared = jnp.concatenate(
        [sums_a[0:1], sums_b[0:1], sums_a[1:2], sums_b[1:2], sums_b[2:4], jnp.zeros((10, D), F32)]
    )
    others = [xor_permute(shared, by) for by in (1, 2, 3)]
    shared = (shared + others[0]) + (others[1] + others[2])
    shared = jnp.concatenate([shared[:, i * LANES : (i + 1) * LANES] for i in range(4)])
    at = 4 * D
    att_own = jnp.concatenate(
        [att_own[:at], (att_own[at : at + 64].astype(F32) + shared).astype(BF), att_own[at + 64 :]]
    )
    pipeline.last = (arrays[DOWN],)
    pipeline.pieces[2] = (att_own, pipeline.pieces[2][1])
    pipeline.advance(6)
    down_slots = gather_slots(pipeline.tied(arrays[DOWN])[0])
    sums = pipeline.finish()

    def spread_images(slots):
        odd, high = tensor % 2 == 1, tensor >= 2
        parts = [part[:PIX] for part in slots]
        pairs = []
        for a, b in (parts[0:2], parts[2:4]):
            pairs.append((jnp.where(odd, b, a), jnp.where(odd, a, b)))
        first = [jnp.where(high, b, a) for a, b in zip(*pairs)]
        second = [jnp.where(high, a, b) for a, b in zip(*pairs)]
        return jnp.stack(first + second)

    section_out = spread_images(out_slots)
    input_grad = spread_images(down_slots).astype(F32)
    fc2_grad, fc1_grad = sums[0].astype(F32), sums[1].astype(F32)
    swapped = odd if lax.axis_size(DP) == 4 else jnp.zeros_like(odd)
    qkv_grad, proj_grad, gains, shifts, biases, fc1_row, qv_rows, table_grad = attention_outputs(
        swapped.astype(jnp.int32).reshape(1), rel_wide, *sums[2]
    )
    outs = (
        section_out,
        input_grad,
        gains,
        shifts,
        qkv_grad.reshape(3, D, LANES),
        qv_rows,
        table_grad,
        proj_grad,
        biases,
        fc1_grad,
        fc1_row.reshape(4 * LANES),
        fc2_grad,
    )
    return tuple(out[None] for out in outs)


def solution(mesh):
    placed = (
        P(DP, None, None),
        P(DP, None, None),
        P(SEC, None, None),
        P(SEC, None, None),
        P(SEC, None, None, TEN),
        P(SEC, None, TEN),
        P(SEC, None, TEN),
        P(SEC, TEN, None),
        P(SEC, None, None),
        P(SEC, None, TEN),
        P(SEC, TEN),
        P(SEC, TEN, None),
        P(),
        P(),
    )
    return jax.shard_map(
        local,
        mesh=mesh,
        in_specs=placed,
        out_specs=(
            P(SEC, DP, None, None),
            P(SEC, DP, None, None),
            P(SEC, None, None),
            P(SEC, None, None),
            P(SEC, None, None, TEN),
            P(SEC, None, TEN),
            P(SEC, None, TEN),
            P(SEC, TEN, None),
            P(SEC, None, None),
            P(SEC, None, TEN),
            P(SEC, TEN),
            P(SEC, TEN, None),
        ),
        check_vma=False,
    )
```

```python
import functools

import jax
import jax.numpy as jnp
import numpy as np
from jax import lax
from jax.experimental import pallas as pl
from jax.experimental.pallas import tpu as pltpu
from jax.sharding import PartitionSpec as P

D = 512
HEAD_DIM = 32
WIN = 7
SIDE = 14
SHIFT = 3
PIX = 196
WTOK = 49
REL = 169
NWIN = 4

ROWS = 64
M = NWIN * ROWS
TOK = 208
GROUP = 4
LANES = GROUP * HEAD_DIM
WIDE = GROUP * ROWS
ATT_SUMS = 3 * D + D + 4 * 16
ATT_ROWS = ATT_SUMS + 2 * ROWS
SLOTS = 4

EPS = 1e-05
SCALE = HEAD_DIM ** (-0.5)
BF = jnp.bfloat16
F32 = jnp.float32
HIGHEST = lax.Precision.HIGHEST

SEC, DP, TEN = "section", "dp", "tensor"

(
    X,
    TILES,
    XHAT1,
    R1,
    NORMED,
    BRANCH,
    MIDDLE,
    XHAT2,
    R2,
    NORMED2,
    RESULT,
    Y,
    GMLP,
    GMIDDLE,
    GBRANCH,
    SUMS_B,
    SUMS_C,
    SUMS_A,
    GTOTAL,
    DOWN,
    ARRIVED,
    UPSTREAM,
    IMAGE,
    PV,
    PERM,
    PERM_T,
    BIAS,
    REGION,
    WA,
    WB,
    QKV,
    PROBS,
    CTX,
    SLOPE,
    HIDDEN,
    GPRE,
    GQKV,
    SCORESUM,
    FC2G,
    FC1G,
    ATTG,
) = range(41)


def dot(a, b, ca, cb):
    return lax.dot_general(a, b, (((ca,), (cb,)), ((), ())), preferred_element_type=F32)


class Env:
    def __init__(self, refs, copies_in, copies_out):
        self.refs, self.copies_in, self.copies_out = refs, dict(copies_in), dict(copies_out)
        self.started = []

    def __getitem__(self, name):
        return self.refs[name]

    def need(self, name):
        for copy in self.copies_in.pop(name, ()):
            copy.wait()
        return self.refs[name]

    def emit(self, name):
        for copy in self.copies_out.pop(name, ()):
            copy.start()
            self.started.append(copy)

    def finish(self):
        for name in list(self.copies_in):
            self.need(name)
        for name in list(self.copies_out):
            self.emit(name)
        for copy in self.started:
            copy.wait()


def head_masks():
    lane = lax.broadcasted_iota(jnp.int32, (1, LANES), 1) // HEAD_DIM
    return [(lane == h).astype(F32) for h in range(GROUP)]


def spread(rows, masks):
    return jnp.concatenate([rows * mask.astype(BF) for mask in masks], axis=0)


def gather_heads(stacked, masks):
    total = stacked[0:ROWS] * masks[0]
    for h in range(1, GROUP):
        total = total + stacked[h * ROWS : (h + 1) * ROWS] * masks[h]
    return total


def norm_of(values):
    center = values - jnp.mean(values, -1, keepdims=True)
    r = lax.rsqrt(jnp.mean(center * center, -1, keepdims=True) + EPS)
    return center * r, r


def qkv_weight_of(ref):
    return jnp.concatenate([ref[i * D : (i + 1) * D] for i in range(3)], axis=1)


def proj_weight_of(ref):
    return jnp.concatenate(
        [ref[3 * D + i * LANES : 3 * D + (i + 1) * LANES] for i in range(D // LANES)], axis=1
    )


def image_norm(env):
    first_norm(env, dot(env[PERM][:, 0:PIX], env.need(IMAGE)[...], 1, 0))


def arrived_norm(env):
    first_norm(env, dot(env[PERM][...], env.need(X)[...], 1, 0))


def first_norm(env, tiles):
    xhat, r = norm_of(tiles)
    env[XHAT1][...] = xhat
    env.emit(XHAT1)
    env[R1][...] = jnp.broadcast_to(r, (M, 128))
    env.emit(R1)
    env[NORMED][...] = (xhat * env[PV][0:1, :] + env[PV][2:3, :]).astype(BF)
    env.emit(NORMED)
    env[BRANCH][...] = tiles + env[PV][4:5, :]


def forward_heads(env, slots):
    masks = head_masks()
    normed = env.need(NORMED)[...]
    branch = env.need(BRANCH)[...]
    regions = [jnp.concatenate([env[REGION][w]] * GROUP, axis=1) for w in range(NWIN)]
    empty = lax.broadcasted_iota(jnp.int32, (ROWS, WIDE), 0) >= WTOK
    for j in slots:
        weights = env.need((WA, j))
        bias = jnp.concatenate([env[BIAS][j * GROUP + h] for h in range(GROUP)], axis=1)
        bias = jnp.where(empty, -1e30, bias)
        packed = dot(normed, qkv_weight_of(weights), 1, 0) + env[PV][12 + j : 13 + j, 0 : 3 * LANES]
        packed = packed.astype(BF)
        env[QKV, j][...] = packed
        env.emit((QKV, j))
        parts = []
        for w in range(NWIN):
            rows = slice(w * ROWS, (w + 1) * ROWS)
            q = packed[rows, 0:LANES]
            k = packed[rows, LANES : 2 * LANES]
            v = packed[rows, 2 * LANES : 3 * LANES]
            scores = dot(k, spread(q, masks), 1, 1) * SCALE + bias + regions[w]
            exps = jnp.exp(scores - jnp.max(scores, 0, keepdims=True))
            probs = exps / jnp.sum(exps, 0, keepdims=True)
            env[PROBS, j][w] = probs
            parts.append(gather_heads(dot(probs.astype(BF), v, 0, 0), masks))
        env.emit((PROBS, j))
        context = jnp.concatenate(parts, axis=0).astype(BF)
        env[CTX, j][...] = context
        env.emit((CTX, j))
        branch = branch + dot(context, proj_weight_of(weights), 1, 0)
    return branch


def forward_near_heads(env):
    env[BRANCH][...] = forward_heads(env, (0, 1))
    env.emit(BRANCH)


def forward_far_heads(env):
    middle = forward_heads(env, (2, 3))
    xhat, r = norm_of(middle)
    env[XHAT2][...] = xhat
    env.emit(XHAT2)
    env[R2][...] = jnp.broadcast_to(r, (M, 128))
    env.emit(R2)
    env[NORMED2][...] = (xhat * env[PV][1:2, :] + env[PV][3:4, :]).astype(BF)
    env.emit(NORMED2)
    env[RESULT][...] = middle + env[PV][5:6, :]


def forward_hidden(env, slots):
    normed = env.need(NORMED2)[...]
    total = env.need(RESULT)[...]
    for j in slots:
        weights = env.need((WB, j))
        pre = dot(normed, weights[0:D], 1, 0) + env[PV][8 + j : 9 + j, :]
        phi = 0.5 * (1.0 + lax.erf(pre * (0.5**0.5)))
        hidden = (pre * phi).astype(BF)
        env[SLOPE, j][...] = phi + pre * jnp.exp(-0.5 * pre * pre) * (2.0 * np.pi) ** -0.5
        env.emit((SLOPE, j))
        env[HIDDEN, j][...] = hidden
        env.emit((HIDDEN, j))
        total = total + dot(hidden, weights[D : 2 * D], 1, 0)
    return total


def forward_near_hidden(env):
    env[RESULT][...] = forward_hidden(env, (0, 1))
    env.emit(RESULT)


def forward_far_hidden(env):
    total = forward_hidden(env, (2, 3))
    env[Y][...] = dot(env[PERM_T][...], total.astype(BF), 1, 0).astype(BF)
    env.emit(Y)


def backward_norm(grad, xhat, r, gain):
    u = grad * gain
    return r * (u - jnp.mean(u, -1, keepdims=True) - xhat * jnp.mean(u * xhat, -1, keepdims=True))


def column_sum(values):
    return jnp.sum(values, 0, keepdims=True)


def backward_mlp(env):
    gmlp = env[GMLP][...]
    gtiles = gmlp.astype(F32)
    sums = env[SUMS_B]
    sums[3:4, :] = column_sum(gtiles)
    total = jnp.zeros((M, D), F32)
    for j in range(SLOTS):
        weights = env.need((WB, j))
        gact = dot(gmlp, weights[D : 2 * D], 1, 1)
        gpre = (gact * env.need((SLOPE, j))[...]).astype(BF)
        env[GPRE, j][...] = gpre
        env.emit((GPRE, j))
        sums[4 + j : 5 + j, :] = column_sum(gpre.astype(F32))
        total = total + dot(gpre, weights[0:D], 1, 1)
    xhat = env.need(XHAT2)[...]
    r = env.need(R2)[:, 0:1]
    sums[0:1, :] = column_sum(total * xhat)
    sums[1:2, :] = column_sum(total)
    gmiddle = gtiles + backward_norm(total, xhat, r, env[PV][1:2, :])
    env[GMIDDLE][...] = gmiddle
    env.emit(GMIDDLE)
    gbranch = gmiddle.astype(BF)
    env[GBRANCH][...] = gbranch
    env.emit(GBRANCH)
    sums[2:3, :] = column_sum(gbranch.astype(F32))
    env.emit(SUMS_B)


def backward_heads(env, slots, total, sums):
    masks = head_masks()
    sums[...] = jnp.zeros_like(sums)
    gbranch = env.need(GBRANCH)[...]
    for j in slots:
        weights = env.need((WA, j))
        gcontext = dot(gbranch, proj_weight_of(weights), 1, 1).astype(BF)
        packed = env.need((QKV, j))[...]
        env.need((PROBS, j))
        score_sum = None
        parts = []
        for w in range(NWIN):
            rows = slice(w * ROWS, (w + 1) * ROWS)
            q = spread(packed[rows, 0:LANES], masks)
            k = packed[rows, LANES : 2 * LANES]
            v = packed[rows, 2 * LANES : 3 * LANES]
            up = spread(gcontext[rows], masks)
            probs = env[PROBS, j][w]
            gprobs = dot(v, up, 1, 1)
            gscores = probs * (gprobs - jnp.sum(gprobs * probs, 0, keepdims=True))
            low = gscores.astype(BF)
            wide = low.astype(F32)
            score_sum = wide if score_sum is None else score_sum + wide
            gv = dot(probs.astype(BF), up, 1, 0)
            gk = dot(low, q, 1, 0) * SCALE
            gq = gather_heads(dot(low, k, 0, 0), masks) * SCALE
            parts.append(jnp.concatenate([gq, gk, gv], axis=1).astype(BF))
        env[SCORESUM, j][...] = score_sum
        env.emit((SCORESUM, j))
        grads = jnp.concatenate(parts, axis=0)
        env[GQKV, j][...] = grads
        env.emit((GQKV, j))
        sums[4 + j : 5 + j, 0 : 3 * LANES] = column_sum(grads.astype(F32))
        total = total + dot(grads, qkv_weight_of(weights), 1, 1)
    return total


def backward_far_heads(env):
    env[GTOTAL][...] = backward_heads(env, (2, 3), jnp.zeros((M, D), F32), env[SUMS_C])
    env.emit(GTOTAL)
    env.emit(SUMS_C)


def backward_near_heads(env):
    sums = env[SUMS_A]
    total = backward_heads(env, (0, 1), env.need(GTOTAL)[...], sums)
    xhat = env.need(XHAT1)[...]
    r = env.need(R1)[:, 0:1]
    sums[0:1, :] = column_sum(total * xhat)
    sums[1:2, :] = column_sum(total)
    sums[2:4, :] = jnp.zeros((2, D), F32)
    env.emit(SUMS_A)
    down = env.need(GMIDDLE)[...] + backward_norm(total, xhat, r, env[PV][0:1, :])
    env[DOWN][...] = dot(env[PERM_T][...], down.astype(BF), 1, 0).astype(BF)
    env.emit(DOWN)


def own_gradient(env):
    env[GMLP][...] = dot(env[PERM][:, 0:PIX], env.need(UPSTREAM)[...], 1, 0).astype(BF)
    env.emit(GMLP)


def arrived_gradient(env):
    env[GMLP][...] = dot(env[PERM][...], env.need(ARRIVED)[...], 1, 0).astype(BF)
    env.emit(GMLP)


ORDER = (3, 1, 2, 0)


def fc2_gradient(env):
    gmlp = env[GMLP][...]
    for j in ORDER:
        env[FC2G, j][...] = dot(env.need((HIDDEN, j))[...], gmlp, 0, 0).astype(BF)
        env.emit((FC2G, j))


def fc1_gradient(env):
    normed = env.need(NORMED2)[...]
    for j in ORDER:
        env[FC1G, j][...] = dot(normed, env.need((GPRE, j))[...], 0, 0).astype(BF)
        env.emit((FC1G, j))


def attention_gradient(env, slots, sums_qv):
    normed = env.need(NORMED)[...]
    gbranch = env.need(GBRANCH)[...]
    sums_b = env.need(SUMS_B)[...]
    sums_qv = env.need(sums_qv)[...]
    for j in slots:
        target = env[ATTG, j]
        grads = dot(normed, env.need((GQKV, j))[...], 0, 0).astype(BF)
        for i in range(3):
            target[i * D : (i + 1) * D, :] = grads[:, i * LANES : (i + 1) * LANES]
        at = 3 * D
        proj = dot(env.need((CTX, j))[...], gbranch, 0, 0).astype(BF)
        small = [jnp.zeros((6, D), F32), sums_b[4 + j : 5 + j], sums_qv[4 + j : 5 + j]]
        small = jnp.concatenate(small + [jnp.zeros((8, D), F32)], axis=0).astype(BF)
        for block in (proj, small, env.need((SCORESUM, j))[...].astype(BF)):
            for i in range(block.shape[1] // LANES):
                count = block.shape[0]
                target[at : at + count, :] = block[:, i * LANES : (i + 1) * LANES]
                at += count
        env.emit((ATTG, j))


def far_attention_gradient(env):
    attention_gradient(env, (3, 2), SUMS_C)


def near_attention_gradient(env):
    attention_gradient(env, (1, 0), SUMS_A)


def shapes_of():
    table = {}
    for name in (X, Y, DOWN, ARRIVED):
        table[name] = ((TOK, D), BF)
    for name in (IMAGE, UPSTREAM):
        table[name] = ((PIX, D), BF)
    for name in (NORMED, NORMED2, GMLP, GBRANCH):
        table[name] = ((M, D), BF)
    for name in (XHAT1, BRANCH, XHAT2, RESULT, GMIDDLE, GTOTAL):
        table[name] = ((M, D), F32)
    for name in (R1, R2):
        table[name] = ((M, 128), F32)
    for name in (SUMS_A, SUMS_B, SUMS_C):
        table[name] = ((8, D), F32)
    for j in range(SLOTS):
        table[WA, j] = ((4 * D, LANES), BF)
        table[WB, j] = ((2 * D, D), BF)
        table[QKV, j] = ((M, 3 * LANES), BF)
        table[PROBS, j] = ((NWIN, ROWS, WIDE), F32)
        table[CTX, j] = ((M, LANES), BF)
        table[SLOPE, j] = ((M, D), F32)
        table[HIDDEN, j] = ((M, D), BF)
        table[GPRE, j] = ((M, D), BF)
        table[GQKV, j] = ((M, 3 * LANES), BF)
        table[SCORESUM, j] = ((ROWS, WIDE), F32)
        table[FC2G, j] = ((D, D), BF)
        table[FC1G, j] = ((D, D), BF)
        table[ATTG, j] = ((ATT_ROWS, LANES), BF)
    return table


SHAPES = shapes_of()
PIECES = {(name, j): 2 for name in (FC2G, FC1G, ATTG) for j in (1, 3)}


def per_slot(*names, slots=range(SLOTS)):
    return [(name, j) for j in slots for name in names]


NEAR, FAR = (0, 1), (2, 3)


def union(lists):
    found = []
    for names in lists:
        found += [name for name in names if name not in found]
    return found


def run_stages(variants, place, small, arrays, keep=(), scratch=()):
    ins = union([variant[2] for variant in variants])
    outs = union([variant[3] for variant in variants])
    local = union([ins, outs, scratch])
    small_names = list(small)
    kept = [name for name in outs if name in keep]
    sources, operands = {}, []
    for name in ins:
        if name in kept:
            continue
        held = arrays[name] if isinstance(arrays[name], list) else [(arrays[name], None)]
        sources[name] = []
        for array, offset in held:
            sources[name].append((len(operands), offset))
            operands.append(array)
    targets, out_shapes = {}, []
    for name in outs:
        shape, dtype = SHAPES[name]
        count = PIECES.get(name, 1)
        targets[name] = list(range(len(out_shapes), len(out_shapes) + count))
        out_shapes += [jax.ShapeDtypeStruct((shape[0] // count,) + shape[1:], dtype)] * count
    n_small, n_in, n_out = len(small_names), len(operands), len(out_shapes)

    def kernel(*refs):
        where = refs[0]
        at = 1
        env_refs = dict(zip(small_names, refs[at : at + n_small]))
        at += n_small
        in_hbm = refs[at : at + n_in]
        at += n_in + len(kept)
        out_hbm = refs[at : at + n_out]
        at += n_out
        env_refs.update(zip(local, refs[at : at + len(local)]))
        sems = refs[at + len(local)]

        def rows_of(name, start, count):
            ref = env_refs[name]
            return ref if start is None else ref.at[pl.ds(start, count)]

        def run(stages, own_ins, own_outs):
            copies_in, copies_out = {}, {}
            for name in own_ins:
                copies_in[name] = []
                if name in kept:
                    held = out_hbm[targets[name][0]]
                    sem = sems.at[n_in + n_out + kept.index(name)]
                    copies_in[name].append(pltpu.make_async_copy(held, env_refs[name], sem))
                    copies_in[name][-1].start()
                    continue
                for i, offset in sources[name]:
                    source = in_hbm[i]
                    if name in (IMAGE, UPSTREAM):
                        source = source.at[where[2]]
                    count = source.shape[0]
                    start = None
                    if callable(offset):
                        start = pl.multiple_of(offset(where), count)
                    elif offset is not None:
                        start = offset
                    part = rows_of(name, start, count)
                    copies_in[name].append(pltpu.make_async_copy(source, part, sems.at[i]))
                    copies_in[name][-1].start()
            for name in own_outs:
                copies_out[name] = []
                for piece, i in enumerate(targets[name]):
                    count = out_hbm[i].shape[0]
                    start = piece * count if len(targets[name]) > 1 else None
                    part = rows_of(name, start, count)
                    copies_out[name].append(
                        pltpu.make_async_copy(part, out_hbm[i], sems.at[n_in + i])
                    )
            env = Env(env_refs, copies_in, copies_out)
            for stage in stages:
                stage(env)
            env.finish()

        for section, stages, own_ins, own_outs in variants:
            body = functools.partial(run, stages, own_ins, own_outs)
            if section is None:
                body()
            else:
                pl.when(where[0] == section)(body)

    vmem = pl.BlockSpec(memory_space=pltpu.VMEM)
    hbm = pl.BlockSpec(memory_space=pltpu.HBM)
    results = pl.pallas_call(
        kernel,
        out_shape=out_shapes,
        in_specs=[pl.BlockSpec(memory_space=pltpu.SMEM)]
        + [vmem] * n_small
        + [hbm] * (n_in + len(kept)),
        out_specs=[hbm] * n_out,
        scratch_shapes=[pltpu.VMEM(*SHAPES[name]) for name in local]
        + [pltpu.SemaphoreType.DMA((n_in + n_out + len(kept),))],
        input_output_aliases={
            1 + n_small + n_in + i: targets[name][0] for i, name in enumerate(kept)
        },
        compiler_params=pltpu.CompilerParams(vmem_limit_bytes=60 * 1024 * 1024),
        cost_estimate=pl.CostEstimate(flops=20_000_000_000, bytes_accessed=10_000, transcendentals=0),
    )(
        place,
        *[small[name] for name in small_names],
        *operands,
        *[arrays[name] for name in kept],
    )
    for name in outs:
        pieces = [results[i] for i in targets[name]]
        arrays[name] = pieces[0] if len(pieces) == 1 else pieces


def attention_outputs(swapped, rel, mine, arriving):
    def kernel(swap, rel, mine, arriving, *refs):
        qkv, proj, gains, shifts, biases, fc1_row, qv_rows, table, bins = refs
        flip = swap[0] == 1
        a, b = mine[...].astype(F32), arriving[...].astype(F32)
        rows = jnp.concatenate([jnp.where(flip, b, a), jnp.where(flip, a, b)], axis=0)
        qkv[...] = rows[: 3 * D]
        for i in range(4):
            lanes = slice(i * LANES, (i + 1) * LANES)
            proj[:, lanes] = rows[3 * D + i * LANES : 3 * D + (i + 1) * LANES]
            small = rows[4 * D + 16 * i : 4 * D + 16 * (i + 1)]
            gains[:, lanes] = small[0:2]
            shifts[:, lanes] = small[2:4]
            biases[:, lanes] = small[4:6]
            fc1_row[:, lanes] = small[6:7]
            if i in (0, 2):
                qv_rows[i // 2 : i // 2 + 1, :] = small[7:8]
        scores = [rows[ATT_SUMS : ATT_SUMS + ROWS], rows[ATT_SUMS + ROWS :]]
        scores = jnp.concatenate(scores, axis=1)
        where = rel[...]

        def eight(i, carry):
            found = [column_sum(jnp.where(where == i * 8 + r, scores, 0.0)) for r in range(8)]
            bins[pl.ds(pl.multiple_of(i * 8, 8), 8), :] = jnp.concatenate(found, axis=0)
            return carry

        bins[...] = jnp.zeros_like(bins)
        lax.fori_loop(0, (REL + 7) // 8, eight, 0)
        head = lax.broadcasted_iota(jnp.int32, (LANES, WIDE), 0)
        pick = (head == lax.broadcasted_iota(jnp.int32, (LANES, WIDE), 1) // ROWS).astype(BF)
        sums = bins[...]
        high = sums.astype(BF)
        sums = dot(high, pick, 1, 1) + dot((sums - high.astype(F32)).astype(BF), pick, 1, 1)
        table[...] = sums[:REL, :GROUP]

    shapes = [(3 * D, LANES), (LANES, D), (2, D), (2, D), (2, D), (1, D), (2, LANES), (REL, GROUP)]
    vmem = pl.BlockSpec(memory_space=pltpu.VMEM)
    return pl.pallas_call(
        kernel,
        out_shape=[jax.ShapeDtypeStruct(shape, F32) for shape in shapes],
        in_specs=[pl.BlockSpec(memory_space=pltpu.SMEM)] + [vmem] * 3,
        out_specs=[vmem] * len(shapes),
        scratch_shapes=[pltpu.VMEM((2 * LANES, WIDE), F32)],
        compiler_params=pltpu.CompilerParams(vmem_limit_bytes=32 * 1024 * 1024),
    )(swapped, rel, mine, arriving)


def tile_places(shift):
    places = np.full((NWIN, ROWS), -1, np.int32)
    for w in range(NWIN):
        for r in range(WTOK):
            i = (w // 2) * WIN + r // WIN
            j = (w % 2) * WIN + r % WIN
            places[w, r] = ((i + shift) % SIDE) * SIDE + (j + shift) % SIDE
    return places.reshape(M)


def permutations(shifted):
    places = jnp.where(shifted, jnp.asarray(tile_places(SHIFT)), jnp.asarray(tile_places(0)))
    tokens = jnp.arange(TOK, dtype=jnp.int32)
    forth = (places[:, None] == tokens[None, :]).astype(BF)
    back = (tokens[:, None] == places[None, :]).astype(BF)
    return forth, back


def region_bias(regions, shifted):
    stripes = SIDE // WIN
    tiled = (
        regions.reshape(stripes, WIN, stripes, WIN)
        .transpose(0, 2, 1, 3)
        .reshape(stripes * stripes, WIN * WIN)
    )
    tiled = jnp.pad(tiled, ((0, 0), (0, ROWS - WTOK)))
    differ = (tiled[:, :, None] != tiled[:, None, :]) & shifted
    return jnp.where(differ, -100.0, 0.0).astype(F32)


def xor_permute(array, by):
    devices = lax.axis_size(TEN)
    return lax.ppermute(array, TEN, [(i, i ^ by) for i in range(devices)])


def gather_slots(array):
    across = xor_permute(array, 2)
    return [array, xor_permute(array, 1), across, xor_permute(across, 1)]


def section_permute(array, source):
    return lax.ppermute(array, SEC, [(source, 1 - source)])


def after(values, *others):
    count = len(values)
    return lax.optimization_barrier(tuple(values) + tuple(others))[:count]


def add_low(a, b):
    return (a.astype(F32) + b.astype(F32)).astype(BF)


class Pipeline:
    order = (
        (0, 0), (0, 1), (1, 0), (1, 1), (2, 0), (0, 2),
        (2, 1), (0, 3), (1, 2), (2, 2), (1, 3), (2, 3),
    )

    def __init__(self):
        self.pieces, self.done, self.last = [], set(), ()
        self.halving = lax.axis_size(DP) == 4
        self.odd = lax.axis_index(DP) % 2 == 1

    def add(self, share, arriving):
        self.pieces.append((share, arriving))

    def events(self):
        return [event for event in self.order if event not in self.done]

    def tied(self, *values):
        return after(values, *self.last)

    def permuted(self, array, by):
        return lax.ppermute(array, DP, [(i, i ^ by) for i in range(4)])

    def advance(self, count):
        if not self.halving:
            return
        for i, stage in self.events()[:count]:
            mine, arriving = self.tied(*self.pieces[i])
            if stage == 0:
                total = add_low(mine, arriving)
                half = total.shape[0] // 2
                low, high = total[:half], total[half:]
                keep = jnp.where(self.odd, high, low)
                send = jnp.where(self.odd, low, high)
                self.last = (keep, send)
                state = (keep, self.permuted(send, 1))
            elif stage < 3:
                total = add_low(mine, arriving)
                self.last = (total,)
                state = (total, self.permuted(total, 3 - stage))
            elif i == 2:
                state = (mine, arriving)
            else:
                low = jnp.where(self.odd, arriving, mine)
                high = jnp.where(self.odd, mine, arriving)
                state = jnp.concatenate([low, high])
                self.last = (arriving,)
            self.done.add((i, stage))
            self.pieces[i] = state

    def finish(self):
        if not self.halving:
            sums = [lax.psum(add_low(*piece), DP) for piece in self.pieces]
            return sums[:2] + [jnp.split(sums[2], 2)]
        self.advance(4 * len(self.pieces))
        return self.pieces


def local(
    images,
    out_grad,
    ln_gain,
    ln_bias,
    qkv_weight,
    qv_bias,
    pos_table,
    proj_weight,
    out_bias,
    fc1_weight,
    fc1_bias,
    fc2_weight,
    rel_index,
    regions,
):
    section = lax.axis_index(SEC)
    shifted = section == 1
    odd = lax.axis_index(DP) % 2
    tensor = lax.axis_index(TEN)
    place = jnp.stack([section, odd, tensor]).astype(jnp.int32)

    arrays = {}
    qkv = qkv_weight[0].reshape(3 * D, LANES)
    proj = proj_weight[0]
    proj = jnp.concatenate([proj[:, i * LANES : (i + 1) * LANES] for i in range(D // LANES)])
    fc1, fc2 = fc1_weight[0], fc2_weight[0]
    quarter = D // 2
    first = jnp.where(odd == 1, jnp.concatenate([qkv[2 * D :], proj]), qkv[: 2 * D])
    chosen = {WA: [first], WB: []}
    for i in range(2):
        rows = slice(i * quarter, (i + 1) * quarter)
        chosen[WB].append(jnp.where(odd == 1, fc2[rows], fc1[rows]))
    arrays[WA, 0] = [(qkv, 0), (proj, 3 * D)]
    arrays[WB, 0] = [(fc1, 0), (fc2, D)]
    pairs = [(i, i ^ 1) for i in range(lax.axis_size(DP))]
    for name, half in ((WA, 2 * D), (WB, D)):
        arrays[name, 1] = [(xor_permute(array, 1), at) for array, at in arrays[name, 0]]
        arrays[name, 2] = []
        for i, part in enumerate(chosen[name]):
            mine = xor_permute(part, 2)
            for array, flip in ((mine, 0), (lax.ppermute(mine, DP, pairs), 1)):

                def offset(where, flip=flip, half=half, start=i * quarter):
                    return (where[1] ^ flip) * half + start

                arrays[name, 2].append((array, offset))

    pad = jnp.zeros((LANES,), F32)
    fc1_bias, qv_bias, pos_table = after((fc1_bias, qv_bias, pos_table), first, *chosen[WB])
    row = jnp.concatenate([qv_bias[0, 0], pad, qv_bias[0, 1], pad])
    table = jnp.pad(pos_table[0].reshape(-1), (0, 2 * D - REL * GROUP)).reshape(2, D)
    own_small = jnp.concatenate([fc1_bias[0][None], row[None], table], axis=0)
    small_slots = gather_slots(own_small)

    def forward_to_core(name, tie=None):
        parts = [array for array, _ in arrays[name, 2]]
        if tie is not None:
            parts[1::2] = after(parts[1::2], tie)
        offsets = [offset for _, offset in arrays[name, 2]]
        arrays[name, 3] = [(xor_permute(part, 1), at) for part, at in zip(parts, offsets)]

    forth, back = permutations(shifted)
    rel = jnp.pad(rel_index, ((0, ROWS - WTOK), (0, ROWS - WTOK)), constant_values=-1)
    onehot = (rel.T[None] == jnp.arange(REL, dtype=jnp.int32)[:, None, None]).astype(BF)
    onehot = onehot.reshape(REL, ROWS * ROWS)
    heads = jnp.stack([part[2:4].reshape(-1)[: REL * GROUP] for part in small_slots])
    heads = heads.reshape(SLOTS, REL, GROUP).transpose(0, 2, 1).reshape(SLOTS * GROUP, REL)
    top = heads.astype(BF)
    mid = (heads - top.astype(F32)).astype(BF)
    end = (heads - top.astype(F32) - mid.astype(F32)).astype(BF)
    bias = dot(jnp.concatenate([top, mid, end]), onehot, 1, 0).reshape(3, SLOTS * GROUP, -1)
    bias = (bias[0] + bias[1] + bias[2]).reshape(SLOTS * GROUP, ROWS, ROWS)
    region = region_bias(regions, shifted)
    vectors = jnp.concatenate(
        [ln_gain[0], ln_bias[0], out_bias[0], jnp.zeros((2, D), F32)]
        + [part[0:1] for part in small_slots]
        + [part[1:2] for part in small_slots],
        axis=0,
    )
    all_small = {PV: vectors, PERM: forth, PERM_T: back, BIAS: bias, REGION: region}
    rel_wide = jnp.tile(rel.T, (1, GROUP))

    def small(*names):
        return {name: all_small[name] for name in names}

    arrays[IMAGE] = [(images, None)]
    arrays[UPSTREAM] = [(out_grad, None)]
    run_stages(
        [(0, [image_norm, forward_near_heads], [IMAGE] + per_slot(WA, slots=NEAR),
          [XHAT1, R1, NORMED, BRANCH] + per_slot(QKV, PROBS, CTX, slots=NEAR))],
        place, small(PV, PERM, BIAS, REGION), arrays,
    )
    forward_to_core(WA, arrays[BRANCH])
    run_stages(
        [(0, [forward_far_heads, forward_near_hidden],
          [NORMED, BRANCH] + per_slot(WA, slots=FAR) + per_slot(WB, slots=NEAR),
          [XHAT2, R2, NORMED2, RESULT] + per_slot(QKV, PROBS, CTX, slots=FAR)
          + per_slot(SLOPE, HIDDEN, slots=NEAR))],
        place, small(PV, BIAS, REGION), arrays,
    )
    forward_to_core(WB, arrays[RESULT])
    run_stages(
        [(0, [forward_far_hidden], [NORMED2, RESULT] + per_slot(WB, slots=FAR),
          [Y] + per_slot(SLOPE, HIDDEN, slots=FAR))],
        place, small(PV, PERM_T), arrays,
    )
    arrays[X] = section_permute(arrays[Y], 0)
    kept = [NORMED, NORMED2, Y] + per_slot(CTX, HIDDEN)
    outs = kept + [GMLP, GBRANCH, SUMS_A, SUMS_B, SUMS_C, DOWN] + per_slot(GPRE, GQKV, SCORESUM)
    stages = [
        arrived_norm,
        forward_near_heads,
        forward_far_heads,
        forward_near_hidden,
        forward_far_hidden,
        own_gradient,
        backward_mlp,
        backward_far_heads,
        backward_near_heads,
    ]
    run_stages(
        [(1, stages, [X] + per_slot(WA) + per_slot(WB) + [UPSTREAM], outs)],
        place, small(PV, PERM, PERM_T, BIAS, REGION), arrays, keep=kept,
        scratch=[XHAT1, R1, BRANCH, XHAT2, R2, RESULT, GMIDDLE, GTOTAL]
        + per_slot(QKV, PROBS, SLOPE),
    )
    across = xor_permute(arrays[Y], 2)
    arrays[ARRIVED], across = after((section_permute(arrays[DOWN], 1), across))
    fc2_out = [GMLP] + per_slot(FC2G)
    run_stages(
        [
            (0, [arrived_gradient, fc2_gradient], [ARRIVED] + per_slot(HIDDEN), fc2_out),
            (1, [own_gradient, fc2_gradient], [UPSTREAM] + per_slot(HIDDEN), fc2_out),
        ],
        place, small(PERM), arrays,
    )

    def to_partners(name):
        far = jnp.concatenate([xor_permute(piece, 1) for piece in arrays[name, 3]])
        own = jnp.concatenate([xor_permute(piece, 1) for piece in arrays[name, 1]])
        return add_low(arrays[name, 2], far), add_low(arrays[name, 0], own)

    fc2_far, fc2_own = to_partners(FC2G)
    gpre, grads = per_slot(GPRE), per_slot(FC1G)
    far_state = per_slot(GQKV, SCORESUM, slots=FAR)
    near_state = per_slot(GQKV, SCORESUM, slots=NEAR)
    far_grads, near_grads = per_slot(ATTG, slots=FAR), per_slot(ATTG, slots=NEAR)
    out_slots = [arrays[Y], xor_permute(arrays[Y], 1), across, xor_permute(across, 1)]
    arrays[ARRIVED], out_slots = after((arrays[ARRIVED], tuple(out_slots)), fc2_far)
    run_stages(
        [
            (0, [arrived_gradient, backward_mlp, fc1_gradient, backward_far_heads, far_attention_gradient],
             [ARRIVED, XHAT2, R2, NORMED2] + per_slot(WB, SLOPE)
             + per_slot(WA, QKV, PROBS, CTX, slots=FAR) + [NORMED],
             gpre + [GMIDDLE, GBRANCH, SUMS_B] + grads + far_state + [SUMS_C, GTOTAL] + far_grads),
            (1, [fc1_gradient, far_attention_gradient],
             [NORMED2] + gpre + [NORMED, GBRANCH, SUMS_B] + per_slot(CTX, slots=FAR)
             + far_state + [SUMS_C],
             grads + far_grads),
        ],
        place, small(PV, PERM), arrays, keep=gpre + [GBRANCH, SUMS_B, SUMS_C] + far_state,
        scratch=[GMLP],
    )
    near_given = [NORMED, GBRANCH, SUMS_B] + per_slot(CTX, slots=NEAR)
    fc1_far, fc1_own = to_partners(FC1G)
    pipeline = Pipeline()
    pipeline.last = (arrays[GTOTAL],)
    pipeline.add(fc2_own, xor_permute(fc2_far, 2))
    pipeline.advance(1)
    far = pipeline.tied(*arrays[ATTG, 3])
    att_far = add_low(arrays[ATTG, 2], jnp.concatenate([xor_permute(piece, 1) for piece in far]))
    pipeline.add(fc1_own, xor_permute(fc1_far, 2))
    pipeline.add(None, xor_permute(att_far, 2))
    arrays[GTOTAL], arrays[SUMS_B] = after((arrays[GTOTAL], arrays[SUMS_B]), fc1_far, att_far)
    run_stages(
        [
            (0, [backward_near_heads, near_attention_gradient],
             near_given + [GTOTAL, XHAT1, R1, GMIDDLE] + per_slot(WA, QKV, PROBS, slots=NEAR),
             near_state + [SUMS_A, DOWN] + near_grads),
            (1, [near_attention_gradient], near_given + near_state + [SUMS_A], near_grads),
        ],
        place, small(PV, PERM_T), arrays, keep=near_state + [SUMS_A, DOWN],
    )
    att_own = add_low(
        arrays[ATTG, 0], jnp.concatenate([xor_permute(piece, 1) for piece in arrays[ATTG, 1]])
    )
    sums_a, sums_b = arrays[SUMS_A], arrays[SUMS_B]
    shared = jnp.concatenate(
        [sums_a[0:1], sums_b[0:1], sums_a[1:2], sums_b[1:2], sums_b[2:4], jnp.zeros((10, D), F32)]
    )
    others = [xor_permute(shared, by) for by in (1, 2, 3)]
    shared = (shared + others[0]) + (others[1] + others[2])
    shared = jnp.concatenate([shared[:, i * LANES : (i + 1) * LANES] for i in range(4)])
    at = 4 * D
    att_own = jnp.concatenate(
        [att_own[:at], (att_own[at : at + 64].astype(F32) + shared).astype(BF), att_own[at + 64 :]]
    )
    pipeline.last = (arrays[DOWN],)
    pipeline.pieces[2] = (att_own, pipeline.pieces[2][1])
    pipeline.advance(6)
    down_slots = gather_slots(pipeline.tied(arrays[DOWN])[0])
    sums = pipeline.finish()

    def spread_images(slots):
        odd, high = tensor % 2 == 1, tensor >= 2
        parts = [part[:PIX] for part in slots]
        pairs = []
        for a, b in (parts[0:2], parts[2:4]):
            pairs.append((jnp.where(odd, b, a), jnp.where(odd, a, b)))
        first = [jnp.where(high, b, a) for a, b in zip(*pairs)]
        second = [jnp.where(high, a, b) for a, b in zip(*pairs)]
        return jnp.stack(first + second)

    section_out = spread_images(out_slots)
    input_grad = spread_images(down_slots).astype(F32)
    fc2_grad, fc1_grad = sums[0].astype(F32), sums[1].astype(F32)
    swapped = odd if lax.axis_size(DP) == 4 else jnp.zeros_like(odd)
    qkv_grad, proj_grad, gains, shifts, biases, fc1_row, qv_rows, table_grad = attention_outputs(
        swapped.astype(jnp.int32).reshape(1), rel_wide, *sums[2]
    )
    outs = (
        section_out,
        input_grad,
        gains,
        shifts,
        qkv_grad.reshape(3, D, LANES),
        qv_rows,
        table_grad,
        proj_grad,
        biases,
        fc1_grad,
        fc1_row.reshape(4 * LANES),
        fc2_grad,
    )
    return tuple(out[None] for out in outs)


def solution(mesh):
    placed = (
        P(DP, None, None),
        P(DP, None, None),
        P(SEC, None, None),
        P(SEC, None, None),
        P(SEC, None, None, TEN),
        P(SEC, None, TEN),
        P(SEC, None, TEN),
        P(SEC, TEN, None),
        P(SEC, None, None),
        P(SEC, None, TEN),
        P(SEC, TEN),
        P(SEC, TEN, None),
        P(),
        P(),
    )
    return jax.shard_map(
        local,
        mesh=mesh,
        in_specs=placed,
        out_specs=(
            P(SEC, DP, None, None),
            P(SEC, DP, None, None),
            P(SEC, None, None),
            P(SEC, None, None),
            P(SEC, None, None, TEN),
            P(SEC, None, TEN),
            P(SEC, None, TEN),
            P(SEC, TEN, None),
            P(SEC, None, None),
            P(SEC, None, TEN),
            P(SEC, TEN),
            P(SEC, TEN, None),
        ),
        check_vma=False,
    )
```
